32 devices in a mesh: replica: 2 (over x), fsdp: 16 (over z, y, core).
Axes of the slice: x: 2, y: 2, z: 4, core: 2. Of those that a mesh axis runs over, the one named last changes fastest.
Arguments:
- counts: int32 [2], P('replica'), may hold values from 100 to 1000
- inner: bfloat16 [2, 3, 2, 8192, 1024], P('replica', None, None, 'fsdp'), may hold values from -6 to 6
- anchor: bfloat16 [3, 2, 8192, 1024], P(None, None, 'fsdp'), may hold values from -6 to 6
- momentum: float32 [3, 2, 8192, 1024], P(None, None, ('fsdp', 'replica')), may hold values from -6 to 6
Outputs:
- new_weights: bfloat16 [3, 2, 8192, 1024], P(None, None, 'fsdp')
- new_momentum: float32 [3, 2, 8192, 1024], P(None, None, ('fsdp', 'replica'))
The draws below stay inside these ranges and needn't reach their ends.
Inputs may be any that keep to these rules, and one draw needn't show every extreme that they name: `counts`: inner steps of a group.
All inputs are finite; a program needn't handle non-finite values.
Results may differ from the reference program's by a relative error of at most 0.001.
Values may be sent and summed in bfloat16 or wider, within the bound.
No kernel may reach another device: no remote copies, remote signals or barrier semaphores. Data moves between devices by JAX's collectives and lax.ppermute only.
A program may use at most 128 MiB of HBM per device.

```python
import jax
import jax.numpy as jnp

D = 8192
KVW = 1024
LAYERS = 3
GROUPS = 2


def block_scale(key, extent, pieces, smallest, top_value):
    def one(position, shards_of):
        steps = jax.random.uniform(jax.random.fold_in(jax.random.fold_in(key, 6), position), (shards_of,), jnp.float32, smallest / len(pieces), top_value / len(pieces))
        return jnp.repeat(jnp.exp(steps), extent[position] // shards_of).reshape((-1,) + (1,) * (len(extent) - position - 1))

    factor_of = one(*pieces[0])
    for cut in pieces[1:]:
        factor_of = factor_of * one(*cut)
    return factor_of


def bell_draw(rng, extent, deviation, reach, split=(), kind=jnp.bfloat16):
    array = deviation * jax.random.normal(rng, extent, jnp.float32)
    if split:
        array = array * block_scale(rng, extent, split, -0.22, 0.18)
    return jnp.clip(array, -reach, reach).astype(kind)


def setup_inputs(seed: int = 0) -> dict:
    streams_of = jax.random.split(jax.random.key(seed), 5)
    return {
        "counts": jax.random.randint(streams_of[0], (GROUPS,), 100, 1001).astype(jnp.int32),
        "inner": bell_draw(streams_of[1], (GROUPS, LAYERS, 2, D, KVW), 1.0, 6.0, ((0, 2), (3, 16))),
        "anchor": bell_draw(streams_of[2], (LAYERS, 2, D, KVW), 1.0, 6.0, ((2, 16),)),
        "momentum": bell_draw(streams_of[3], (LAYERS, 2, D, KVW), 1.0, 6.0, ((2, 32),), jnp.float32),
    }


outer_rate = 0.7
momentum_rate = 0.9


def reference(counts, inner, anchor, momentum):
    weights = counts.astype(jnp.float32)
    total = jnp.sum(weights)
    base = anchor.astype(jnp.float32)
    acc = jnp.zeros(anchor.shape, jnp.float32)
    for group in range(GROUPS):
        acc = acc + weights[group] * (base - inner[group].astype(jnp.float32))
    pseudo = acc / total
    new_momentum = momentum_rate * momentum + pseudo
    new_weights = (base - outer_rate * (pseudo + momentum_rate * new_momentum)).astype(jnp.bfloat16)
    return new_weights, new_momentum
```

```python
import jax
import jax.numpy as jnp
from jax import lax
from jax.sharding import PartitionSpec as P

outer_rate = 0.7
momentum_rate = 0.9


def solution(mesh):
    groups = mesh.shape["replica"]

    def shifted(value, shift):
        pairs = [(i, (i + shift) % groups) for i in range(groups)]
        return lax.ppermute(value, "replica", pairs)

    def on_device(counts, inner, anchor, momentum):
        layers, kinds, owned = momentum.shape[:3]
        me = lax.axis_index("replica")
        start = me * owned
        parts = [(i, j) for i in range(layers) for j in range(kinds)]
        mine = counts[0].astype(jnp.float32)
        others = [shifted(counts, s)[0].astype(jnp.float32) for s in range(1, groups)]
        total = mine + sum(others)

        def rows(array, part, at):
            return lax.dynamic_slice_in_dim(array[part], at * owned, owned, 0)

        arrived = {}
        for part in parts:
            arrived[part] = [
                shifted(rows(inner[0], part, (me + s) % groups), s) for s in range(1, groups)
            ]
        weights = jnp.zeros(anchor.shape, jnp.bfloat16)
        moments = jnp.zeros(momentum.shape, jnp.float32)
        for part in parts:
            base = rows(anchor, part, me).astype(jnp.float32)
            acc = mine * (base - rows(inner[0], part, me).astype(jnp.float32))
            for count, block in zip(others, arrived[part]):
                acc = acc + count * (base - block.astype(jnp.float32))
            pseudo = acc / total
            moment = momentum_rate * momentum[part] + pseudo
            new = (base - outer_rate * (pseudo + momentum_rate * moment)).astype(jnp.bfloat16)
            moments = moments.at[part].set(moment)
            weights = lax.dynamic_update_slice(weights, new[None, None], (*part, start, 0))
            for s in range(1, groups):
                block = shifted(new, s)
                source = (me - s) % groups
                weights = lax.dynamic_update_slice(
                    weights, block[None, None], (*part, source * owned, 0)
                )
        return weights, moments

    placed = (
        P("replica"),
        P("replica", None, None, "fsdp", None),
        P(None, None, "fsdp", None),
        P(None, None, ("fsdp", "replica"), None),
    )
    return jax.shard_map(
        on_device,
        mesh=mesh,
        in_specs=placed,
        out_specs=(P(None, None, "fsdp", None), P(None, None, ("fsdp", "replica"), None)),
        check_vma=False,
    )
```

```python
import jax
import jax.numpy as jnp
from jax import lax
from jax.sharding import PartitionSpec as P

outer_rate = 0.7
momentum_rate = 0.9


def solution(mesh):
    groups = mesh.shape["replica"]

    def shifted(value, shift):
        pairs = [(i, (i + shift) % groups) for i in range(groups)]
        return lax.ppermute(value, "replica", pairs)

    def on_device(counts, inner, anchor, momentum):
        layers, kinds, owned = momentum.shape[:3]
        me = lax.axis_index("replica")
        start = me * owned
        parts = [(i, j) for i in range(layers) for j in range(kinds)]
        mine = counts[0].astype(jnp.float32)
        others = [shifted(counts, s)[0].astype(jnp.float32) for s in range(1, groups)]
        total = mine + sum(others)

        def rows(array, part, at):
            lead = (0,) * (array.ndim - 4)
            sizes = (1,) * (array.ndim - 2) + (owned, array.shape[-1])
            block = lax.dynamic_slice(array, (*lead, *part, at * owned, 0), sizes)
            return block.reshape(sizes[-2:])

        arrived = {
            part: [shifted(rows(inner, part, (me + s) % groups), s) for s in range(1, groups)]
            for part in parts
        }
        weights = jnp.zeros(anchor.shape, jnp.bfloat16)
        moments = jnp.zeros(momentum.shape, jnp.float32)
        travelled = {}
        for part in parts:
            base = rows(anchor, part, me).astype(jnp.float32)
            acc = mine * (base - rows(inner, part, me).astype(jnp.float32))
            for count, block in zip(others, arrived[part]):
                acc = acc + count * (base - block.astype(jnp.float32))
            pseudo = acc / total
            moment = momentum_rate * momentum[part] + pseudo
            new = (base - outer_rate * (pseudo + momentum_rate * moment)).astype(jnp.bfloat16)
            moments = moments.at[part].set(moment)
            weights = lax.dynamic_update_slice(weights, new[None, None], (*part, start, 0))
            travelled[part] = [shifted(new, s) for s in range(1, groups)]
        for part in parts:
            for s, block in enumerate(travelled[part], 1):
                source = (me - s) % groups
                weights = lax.dynamic_update_slice(
                    weights, block[None, None], (*part, source * owned, 0)
                )
        return weights, moments

    placed = (
        P("replica"),
        P("replica", None, None, "fsdp", None),
        P(None, None, "fsdp", None),
        P(None, None, ("fsdp", "replica"), None),
    )
    return jax.shard_map(
        on_device,
        mesh=mesh,
        in_specs=placed,
        out_specs=(P(None, None, "fsdp", None), P(None, None, ("fsdp", "replica"), None)),
        check_vma=False,
    )
```

```python
import functools

import jax
import jax.numpy as jnp
from jax import lax
from jax.experimental import pallas as pl
from jax.experimental.pallas import tpu as pltpu
from jax.sharding import PartitionSpec as P

outer_rate = 0.7
momentum_rate = 0.9
vmem_bytes = 48 * 1024 * 1024


def update_kernel(groups, me_ref, mine_ref, *refs):
    others, refs = refs[: groups - 1], refs[groups - 1 :]
    anchor_ref, inner_ref, refs = refs[0], refs[1], refs[2:]
    arrived, refs = refs[: groups - 1], refs[groups - 1 :]
    momentum_ref, refs = refs[0], refs[1:]
    new_ref, weights_ref, moments_ref = refs[-3:]
    base = anchor_ref[...].astype(jnp.float32)
    mine = mine_ref[0].astype(jnp.float32)
    total = mine
    acc = mine * (base - inner_ref[...].astype(jnp.float32))
    for count_ref, block_ref in zip(others, arrived):
        count = count_ref[0].astype(jnp.float32)
        total = total + count
        acc = acc + count * (base - block_ref[...].astype(jnp.float32))
    pseudo = acc / total
    moment = momentum_rate * momentum_ref[...] + pseudo
    new = (base - outer_rate * (pseudo + momentum_rate * moment)).astype(jnp.bfloat16)
    moments_ref[...] = moment
    weights_ref[...] = new
    new_ref[...] = new


def update(groups, chunk, me, counts, anchor, inner, arrived, momentum, held):
    lo, hi = chunk
    parts, owned, width = momentum.shape
    rows = min(owned, 128)
    steps = owned // rows
    block = (1, rows, width)
    scalar = pl.BlockSpec(memory_space=pltpu.SMEM)
    spread = pl.BlockSpec(block, lambda p, r, me_ref: (lo + p, me_ref[0] * steps + r, 0))
    packed = pl.BlockSpec(block, lambda p, r, me_ref: (p, r, 0))
    kept = pl.BlockSpec(block, lambda p, r, me_ref: (lo + p, r, 0))
    aliases = {}
    if held:
        first = 1 + groups + 2 + (groups - 1) + 1
        aliases = {first: 1, first + 1: 2}
    size = (hi - lo) * owned * width
    return pl.pallas_call(
        functools.partial(update_kernel, groups),
        grid_spec=pltpu.PrefetchScalarGridSpec(
            num_scalar_prefetch=1,
            grid=(hi - lo, steps),
            in_specs=[scalar] * groups
            + [spread, spread]
            + [packed] * (groups - 1)
            + [kept]
            + [pl.BlockSpec(memory_space=pl.ANY)] * len(held),
            out_specs=[packed, spread, kept],
        ),
        out_shape=[
            jax.ShapeDtypeStruct((hi - lo, owned, width), jnp.bfloat16),
            jax.ShapeDtypeStruct(anchor.shape, jnp.bfloat16),
            jax.ShapeDtypeStruct(momentum.shape, jnp.float32),
        ],
        input_output_aliases=aliases,
        compiler_params=pltpu.CompilerParams(vmem_limit_bytes=vmem_bytes),
        cost_estimate=pl.CostEstimate(
            flops=12 * size, bytes_accessed=(14 + 2 * groups) * size, transcendentals=0
        ),
        name="update",
    )(me, *counts, anchor, inner, *arrived, momentum, *held)


def place_kernel(lo, at_ref, block_ref, _, weights_ref, sem):
    parts, owned, _ = block_ref.shape
    start = pl.multiple_of(at_ref[0] * owned, owned)
    copy = pltpu.make_async_copy(
        block_ref, weights_ref.at[pl.ds(lo, parts), pl.ds(start, owned), :], sem
    )
    copy.start()
    copy.wait()


def place(chunk, at, block, weights):
    anywhere = pl.BlockSpec(memory_space=pl.ANY)
    return pl.pallas_call(
        functools.partial(place_kernel, chunk[0]),
        in_specs=[pl.BlockSpec(memory_space=pltpu.SMEM), anywhere, anywhere],
        out_specs=anywhere,
        out_shape=jax.ShapeDtypeStruct(weights.shape, weights.dtype),
        scratch_shapes=[pltpu.SemaphoreType.DMA],
        input_output_aliases={2: 0},
        compiler_params=pltpu.CompilerParams(vmem_limit_bytes=vmem_bytes),
        cost_estimate=pl.CostEstimate(flops=0, bytes_accessed=4 * block.size, transcendentals=0),
        name="place",
    )(at, block, weights)


def solution(mesh):
    groups = mesh.shape["replica"]

    def shifted(value, shift):
        pairs = [(i, (i + shift) % groups) for i in range(groups)]
        return lax.ppermute(value, "replica", pairs)

    def on_device(counts, inner, anchor, momentum):
        shape = anchor.shape
        owned, width = momentum.shape[-2:]
        parts = shape[0] * shape[1]
        inner = inner.reshape(parts, *shape[-2:])
        anchor = anchor.reshape(parts, *shape[-2:])
        momentum = momentum.reshape(parts, owned, width)
        me = lax.axis_index("replica")
        chunks = [(p, p + 1) for p in range(parts)]
        shifts = range(1, groups)

        def rows_for(array, chunk, target):
            sizes = (chunk[1] - chunk[0], owned, width)
            return lax.dynamic_slice(array, (chunk[0], target * owned, 0), sizes)

        targets = [(me + s) % groups for s in shifts]
        first = [rows_for(inner, chunks[0], t) for t in targets]
        first, rest = lax.optimization_barrier((first, inner))
        sent = [first] + [[rows_for(rest, c, t) for t in targets] for c in chunks[1:]]
        arrived = [[shifted(v, s) for v, s in zip(values, shifts)] for values in sent]
        all_counts = [counts] + [shifted(counts, s) for s in shifts]

        where = me.reshape(1).astype(jnp.int32)
        held = []
        travelled = []
        for chunk, blocks in zip(chunks, arrived):
            new, *held = update(
                groups, chunk, where, all_counts, anchor, inner, blocks, momentum, held
            )
            travelled.append([shifted(new, s) for s in shifts])
        weights, moments = held
        for chunk, blocks in zip(chunks, travelled):
            for s, block in zip(shifts, blocks):
                source = ((me - s) % groups).reshape(1).astype(jnp.int32)
                weights = place(chunk, source, block, weights)
        return weights.reshape(shape), moments.reshape(*shape[:2], owned, width)

    placed = (
        P("replica"),
        P("replica", None, None, "fsdp", None),
        P(None, None, "fsdp", None),
        P(None, None, ("fsdp", "replica"), None),
    )
    return jax.shard_map(
        on_device,
        mesh=mesh,
        in_specs=placed,
        out_specs=(P(None, None, "fsdp", None), P(None, None, ("fsdp", "replica"), None)),
        check_vma=False,
    )
```

```python
import functools

import jax
import jax.numpy as jnp
from jax import lax
from jax.experimental import pallas as pl
from jax.experimental.pallas import tpu as pltpu
from jax.sharding import PartitionSpec as P

outer_rate = 0.7
momentum_rate = 0.9
vmem_bytes = 48 * 1024 * 1024


def share_kernel(*refs):
    counts, shares_ref = refs[:-1], refs[-1]
    values = [ref[0].astype(jnp.float32) for ref in counts]
    total = values[0]
    for value in values[1:]:
        total = total + value
    for g, value in enumerate(values):
        shares_ref[g] = value / total


def share(counts):
    scalar = pl.BlockSpec(memory_space=pltpu.SMEM)
    return pl.pallas_call(
        share_kernel,
        in_specs=[scalar] * len(counts),
        out_specs=scalar,
        out_shape=jax.ShapeDtypeStruct((len(counts),), jnp.float32),
        name="share",
    )(*counts)


def update_kernel(groups, me_ref, shares_ref, anchor_ref, inner_ref, *refs):
    arrived, momentum_ref = refs[: groups - 1], refs[groups - 1]
    new_ref, weights_ref, moments_ref = refs[-3:]
    base = anchor_ref[...].astype(jnp.float32)
    pseudo = shares_ref[0] * (base - inner_ref[...].astype(jnp.float32))
    for g, block_ref in enumerate(arrived, 1):
        pseudo = pseudo + shares_ref[g] * (base - block_ref[...].astype(jnp.float32))
    moment = momentum_rate * momentum_ref[...] + pseudo
    new = (base - outer_rate * (pseudo + momentum_rate * moment)).astype(jnp.bfloat16)
    moments_ref[...] = moment
    weights_ref[...] = new
    new_ref[...] = new


def update(groups, chunk, me, shares, anchor, inner, arrived, momentum, held):
    lo, hi = chunk
    parts, owned, width = momentum.shape
    rows = min(owned, 128)
    steps = owned // rows
    block = (1, rows, width)
    scalar = pl.BlockSpec(memory_space=pltpu.SMEM)
    spread = pl.BlockSpec(block, lambda p, r, me_ref: (lo + p, me_ref[0] * steps + r, 0))
    packed = pl.BlockSpec(block, lambda p, r, me_ref: (p, r, 0))
    kept = pl.BlockSpec(block, lambda p, r, me_ref: (lo + p, r, 0))
    aliases = {groups + 4: 1, groups + 5: 2} if held else {}
    size = (hi - lo) * owned * width
    return pl.pallas_call(
        functools.partial(update_kernel, groups),
        grid_spec=pltpu.PrefetchScalarGridSpec(
            num_scalar_prefetch=1,
            grid=(hi - lo, steps),
            in_specs=[scalar, spread, spread]
            + [packed] * (groups - 1)
            + [kept]
            + [pl.BlockSpec(memory_space=pl.ANY)] * len(held),
            out_specs=[packed, spread, kept],
        ),
        out_shape=[
            jax.ShapeDtypeStruct((hi - lo, owned, width), jnp.bfloat16),
            jax.ShapeDtypeStruct(anchor.shape, jnp.bfloat16),
            jax.ShapeDtypeStruct(momentum.shape, jnp.float32),
        ],
        input_output_aliases=aliases,
        compiler_params=pltpu.CompilerParams(vmem_limit_bytes=vmem_bytes),
        cost_estimate=pl.CostEstimate(
            flops=12 * size, bytes_accessed=(14 + 2 * groups) * size, transcendentals=0
        ),
        name="update",
    )(me, shares, anchor, inner, *arrived, momentum, *held)


def place_kernel(lo, at_ref, block_ref, _, weights_ref, sem):
    parts, owned, _ = block_ref.shape
    start = pl.multiple_of(at_ref[0] * owned, owned)
    copy = pltpu.make_async_copy(
        block_ref, weights_ref.at[pl.ds(lo, parts), pl.ds(start, owned), :], sem
    )
    copy.start()
    copy.wait()


def place(chunk, at, block, weights):
    anywhere = pl.BlockSpec(memory_space=pl.ANY)
    return pl.pallas_call(
        functools.partial(place_kernel, chunk[0]),
        in_specs=[pl.BlockSpec(memory_space=pltpu.SMEM), anywhere, anywhere],
        out_specs=anywhere,
        out_shape=jax.ShapeDtypeStruct(weights.shape, weights.dtype),
        scratch_shapes=[pltpu.SemaphoreType.DMA],
        input_output_aliases={2: 0},
        compiler_params=pltpu.CompilerParams(vmem_limit_bytes=vmem_bytes),
        cost_estimate=pl.CostEstimate(flops=0, bytes_accessed=4 * block.size, transcendentals=0),
        name="place",
    )(at, block, weights)


def solution(mesh):
    groups = mesh.shape["replica"]

    def shifted(value, shift):
        pairs = [(i, (i + shift) % groups) for i in range(groups)]
        return lax.ppermute(value, "replica", pairs)

    def on_device(counts, inner, anchor, momentum):
        shape = anchor.shape
        owned, width = momentum.shape[-2:]
        parts = shape[0] * shape[1]
        inner = inner.reshape(parts, *shape[-2:])
        anchor = anchor.reshape(parts, *shape[-2:])
        momentum = momentum.reshape(parts, owned, width)
        me = lax.axis_index("replica")
        chunks = [(p, p + 1) for p in range(parts)]
        shifts = range(1, groups)

        def rows_for(array, chunk, target):
            sizes = (chunk[1] - chunk[0], owned, width)
            return lax.dynamic_slice(array, (chunk[0], target * owned, 0), sizes)

        other_counts = [shifted(counts, s) for s in shifts]
        targets = [(me + s) % groups for s in shifts]
        first = [rows_for(inner, chunks[0], t) for t in targets]
        first, rest, other_counts = lax.optimization_barrier((first, inner, other_counts))
        shares = share([counts] + other_counts)
        sent = [first] + [[rows_for(rest, c, t) for t in targets] for c in chunks[1:]]
        arrived = [[shifted(v, s) for v, s in zip(values, shifts)] for values in sent]

        where = me.reshape(1).astype(jnp.int32)
        held = []
        travelled = []
        for chunk, blocks in zip(chunks, arrived):
            new, *held = update(
                groups, chunk, where, shares, anchor, inner, blocks, momentum, held
            )
            travelled.append([shifted(new, s) for s in shifts])
        weights, moments = held
        for chunk, blocks in zip(chunks, travelled):
            for s, block in zip(shifts, blocks):
                source = ((me - s) % groups).reshape(1).astype(jnp.int32)
                weights = place(chunk, source, block, weights)
        return weights.reshape(shape), moments.reshape(*shape[:2], owned, width)

    placed = (
        P("replica"),
        P("replica", None, None, "fsdp", None),
        P(None, None, "fsdp", None),
        P(None, None, ("fsdp", "replica"), None),
    )
    return jax.shard_map(
        on_device,
        mesh=mesh,
        in_specs=placed,
        out_specs=(P(None, None, "fsdp", None), P(None, None, ("fsdp", "replica"), None)),
        check_vma=False,
    )
```

```python
import functools

import jax
import jax.numpy as jnp
from jax import lax
from jax.experimental import pallas as pl
from jax.experimental.pallas import tpu as pltpu
from jax.sharding import PartitionSpec as P

outer_rate = 0.7
momentum_rate = 0.9
lanes = 128
spare = 16
vmem_bytes = 48 * 1024 * 1024


def pack_kernel(target_ref, count_ref, inner_ref, out_ref, tile_ref, sems):
    owned = (out_ref.shape[0] - spare) // (inner_ref.shape[2] // lanes)
    start = pl.multiple_of(target_ref[0] * owned, owned)
    copies = [
        pltpu.make_async_copy(
            inner_ref.at[0, pl.ds(start, owned), pl.ds(j * lanes, lanes)],
            out_ref.at[pl.ds(j * owned, owned), :],
            sems.at[j],
        )
        for j in range(inner_ref.shape[2] // lanes)
    ]
    for copy in copies:
        copy.start()
    count = count_ref[0]
    high = (count >> 8).astype(jnp.float32)
    low = (count & 255).astype(jnp.float32)
    row = lax.broadcasted_iota(jnp.int32, tile_ref.shape, 0)
    tile_ref[...] = jnp.where(row == 0, high, low).astype(jnp.bfloat16)
    copies.append(
        pltpu.make_async_copy(
            tile_ref,
            out_ref.at[pl.ds(out_ref.shape[0] - spare, spare), :],
            sems.at[len(copies)],
        )
    )
    copies[-1].start()
    for copy in copies:
        copy.wait()


def pack(target, counts, inner, owned):
    blocks = inner.shape[2] // lanes
    scalar = pl.BlockSpec(memory_space=pltpu.SMEM)
    anywhere = pl.BlockSpec(memory_space=pl.ANY)
    return pl.pallas_call(
        pack_kernel,
        in_specs=[scalar, scalar, anywhere],
        out_specs=anywhere,
        out_shape=jax.ShapeDtypeStruct((blocks * owned + spare, lanes), jnp.bfloat16),
        scratch_shapes=[
            pltpu.VMEM((spare, lanes), jnp.bfloat16),
            pltpu.SemaphoreType.DMA((blocks + 1,)),
        ],
        compiler_params=pltpu.CompilerParams(vmem_limit_bytes=vmem_bytes),
        cost_estimate=pl.CostEstimate(
            flops=0, bytes_accessed=4 * blocks * owned * lanes, transcendentals=0
        ),
        name="pack",
    )(target, counts, inner)


def share_kernel(mine_ref, *refs):
    tiles, shares_ref = refs[:-1], refs[-1]
    values = [mine_ref[0].astype(jnp.float32)]
    for ref in tiles:
        tile = ref[...].astype(jnp.float32)
        values.append(tile[0, 0] * 256.0 + tile[1, 0])
    total = values[0]
    for value in values[1:]:
        total = total + value
    for g, value in enumerate(values):
        shares_ref[g] = value / total


def share(counts, arrived):
    scalar = pl.BlockSpec(memory_space=pltpu.SMEM)
    last = arrived[0].shape[0] // spare - 1
    tile = pl.BlockSpec((spare, lanes), lambda i: (last, 0))
    return pl.pallas_call(
        share_kernel,
        grid=(1,),
        in_specs=[scalar] + [tile] * len(arrived),
        out_specs=scalar,
        out_shape=jax.ShapeDtypeStruct((1 + len(arrived),), jnp.float32),
        name="share",
    )(counts, *arrived)


def update_kernel(groups, me_ref, shares_ref, anchor_ref, inner_ref, *refs):
    arrived, momentum_ref = refs[: groups - 1], refs[groups - 1]
    new_ref, weights_ref, moments_ref = refs[-3:]
    base = anchor_ref[...].astype(jnp.float32)
    pseudo = shares_ref[0] * (base - inner_ref[...].astype(jnp.float32))
    for g, block_ref in enumerate(arrived, 1):
        block = block_ref[...].astype(jnp.float32).reshape(base.shape)
        pseudo = pseudo + shares_ref[g] * (base - block)
    moment = momentum_rate * momentum_ref[...] + pseudo
    new = (base - outer_rate * (pseudo + momentum_rate * moment)).astype(jnp.bfloat16)
    moments_ref[...] = moment
    weights_ref[...] = new
    new_ref[...] = new


def update(groups, chunk, me, shares, anchor, inner, arrived, momentum, held):
    lo, hi = chunk
    parts, owned, width = momentum.shape
    if held:
        rows = min(owned, 128)
        steps = owned // rows
        grid = (hi - lo, steps)
        block = (1, rows, width)
        came = pl.BlockSpec(block, lambda p, r, me_ref: (p, r, 0))
        packed = came
        spread = pl.BlockSpec(block, lambda p, r, me_ref: (lo + p, me_ref[0] * steps + r, 0))
        kept = pl.BlockSpec(block, lambda p, r, me_ref: (lo + p, r, 0))
    else:
        grid = (1, width // lanes)
        block = (1, owned, lanes)
        came = pl.BlockSpec((owned, lanes), lambda p, j, me_ref: (j, 0))
        packed = pl.BlockSpec(block, lambda p, j, me_ref: (0, 0, j))
        spread = pl.BlockSpec(block, lambda p, j, me_ref: (lo, me_ref[0], j))
        kept = pl.BlockSpec(block, lambda p, j, me_ref: (lo, 0, j))
    scalar = pl.BlockSpec(memory_space=pltpu.SMEM)
    aliases = {groups + 4: 1, groups + 5: 2} if held else {}
    size = (hi - lo) * owned * width
    return pl.pallas_call(
        functools.partial(update_kernel, groups),
        grid_spec=pltpu.PrefetchScalarGridSpec(
            num_scalar_prefetch=1,
            grid=grid,
            in_specs=[scalar, spread, spread]
            + [came] * (groups - 1)
            + [kept]
            + [pl.BlockSpec(memory_space=pl.ANY)] * len(held),
            out_specs=[packed, spread, kept],
        ),
        out_shape=[
            jax.ShapeDtypeStruct((hi - lo, owned, width), jnp.bfloat16),
            jax.ShapeDtypeStruct(anchor.shape, jnp.bfloat16),
            jax.ShapeDtypeStruct(momentum.shape, jnp.float32),
        ],
        input_output_aliases=aliases,
        compiler_params=pltpu.CompilerParams(vmem_limit_bytes=vmem_bytes),
        cost_estimate=pl.CostEstimate(
            flops=12 * size, bytes_accessed=(14 + 2 * groups) * size, transcendentals=0
        ),
        name="update",
    )(me, shares, anchor, inner, *arrived, momentum, *held)


def place_kernel(lo, at_ref, block_ref, _, weights_ref, sem):
    parts, owned, _ = block_ref.shape
    start = pl.multiple_of(at_ref[0] * owned, owned)
    copy = pltpu.make_async_copy(
        block_ref, weights_ref.at[pl.ds(lo, parts), pl.ds(start, owned), :], sem
    )
    copy.start()
    copy.wait()


def place(chunk, at, block, weights):
    anywhere = pl.BlockSpec(memory_space=pl.ANY)
    return pl.pallas_call(
        functools.partial(place_kernel, chunk[0]),
        in_specs=[pl.BlockSpec(memory_space=pltpu.SMEM), anywhere, anywhere],
        out_specs=anywhere,
        out_shape=jax.ShapeDtypeStruct(weights.shape, weights.dtype),
        scratch_shapes=[pltpu.SemaphoreType.DMA],
        input_output_aliases={2: 0},
        compiler_params=pltpu.CompilerParams(vmem_limit_bytes=vmem_bytes),
        cost_estimate=pl.CostEstimate(flops=0, bytes_accessed=4 * block.size, transcendentals=0),
        name="place",
    )(at, block, weights)


def solution(mesh):
    groups = mesh.shape["replica"]

    def shifted(value, shift):
        pairs = [(i, (i + shift) % groups) for i in range(groups)]
        return lax.ppermute(value, "replica", pairs)

    def on_device(counts, inner, anchor, momentum):
        shape = anchor.shape
        owned, width = momentum.shape[-2:]
        parts = shape[0] * shape[1]
        inner = inner.reshape(parts, *shape[-2:])
        anchor = anchor.reshape(parts, *shape[-2:])
        momentum = momentum.reshape(parts, owned, width)
        me = lax.axis_index("replica")
        chunks = [(p, p + 1) for p in range(parts)]
        shifts = range(1, groups)

        def rows_for(array, chunk, target):
            sizes = (chunk[1] - chunk[0], owned, width)
            return lax.dynamic_slice(array, (chunk[0], target * owned, 0), sizes)

        targets = [(me + s) % groups for s in shifts]
        first = [pack(t.reshape(1).astype(jnp.int32), counts, inner, owned) for t in targets]
        first, rest = lax.optimization_barrier((first, inner))
        sent = [first] + [[rows_for(rest, c, t) for t in targets] for c in chunks[1:]]
        arrived = [[shifted(v, s) for v, s in zip(values, shifts)] for values in sent]
        shares = share(counts, arrived[0])

        where = me.reshape(1).astype(jnp.int32)
        held = []
        travelled = []
        for chunk, blocks in zip(chunks, arrived):
            new, *held = update(
                groups, chunk, where, shares, anchor, inner, blocks, momentum, held
            )
            travelled.append([shifted(new, s) for s in shifts])
        weights, moments = held
        for chunk, blocks in zip(chunks, travelled):
            for s, block in zip(shifts, blocks):
                source = ((me - s) % groups).reshape(1).astype(jnp.int32)
                weights = place(chunk, source, block, weights)
        return weights.reshape(shape), moments.reshape(*shape[:2], owned, width)

    placed = (
        P("replica"),
        P("replica", None, None, "fsdp", None),
        P(None, None, "fsdp", None),
        P(None, None, ("fsdp", "replica"), None),
    )
    return jax.shard_map(
        on_device,
        mesh=mesh,
        in_specs=placed,
        out_specs=(P(None, None, "fsdp", None), P(None, None, ("fsdp", "replica"), None)),
        check_vma=False,
    )
```

```python
import functools
import math
from typing import NamedTuple

import jax
import jax.numpy as jnp
from jax import lax
from jax.experimental import pallas as pl
from jax.experimental.pallas import tpu as pltpu
from jax.sharding import PartitionSpec as P

outer_rate = 0.7
momentum_rate = 0.9
lanes = 128
spare = 16
vmem_bytes = 48 * 1024 * 1024


class Chunk(NamedTuple):
    lo: int
    parts: int
    row: int
    rows: int


def pack_kernel(owned, part, row, target_ref, count_ref, inner_ref, out_ref, tile_ref, sems):
    rows = (out_ref.shape[0] - spare) // (inner_ref.shape[2] // lanes)
    start = pl.multiple_of(target_ref[0] * owned + row, spare)
    copies = [
        pltpu.make_async_copy(
            inner_ref.at[part, pl.ds(start, rows), pl.ds(j * lanes, lanes)],
            out_ref.at[pl.ds(j * rows, rows), :],
            sems.at[j],
        )
        for j in range(inner_ref.shape[2] // lanes)
    ]
    for copy in copies:
        copy.start()
    count = count_ref[0]
    high = (count >> 8).astype(jnp.float32)
    low = (count & 255).astype(jnp.float32)
    row = lax.broadcasted_iota(jnp.int32, tile_ref.shape, 0)
    tile_ref[...] = jnp.where(row == 0, high, low).astype(jnp.bfloat16)
    copies.append(
        pltpu.make_async_copy(
            tile_ref,
            out_ref.at[pl.ds(out_ref.shape[0] - spare, spare), :],
            sems.at[len(copies)],
        )
    )
    copies[-1].start()
    for copy in copies:
        copy.wait()


def pack(chunk, target, counts, inner, owned):
    part, row, rows = chunk.lo, chunk.row, chunk.rows
    blocks = inner.shape[2] // lanes
    scalar = pl.BlockSpec(memory_space=pltpu.SMEM)
    anywhere = pl.BlockSpec(memory_space=pl.ANY)
    return pl.pallas_call(
        functools.partial(pack_kernel, owned, part, row),
        in_specs=[scalar, scalar, anywhere],
        out_specs=anywhere,
        out_shape=jax.ShapeDtypeStruct((blocks * rows + spare, lanes), jnp.bfloat16),
        scratch_shapes=[
            pltpu.VMEM((spare, lanes), jnp.bfloat16),
            pltpu.SemaphoreType.DMA((blocks + 1,)),
        ],
        compiler_params=pltpu.CompilerParams(vmem_limit_bytes=vmem_bytes),
        cost_estimate=pl.CostEstimate(
            flops=0, bytes_accessed=4 * blocks * rows * lanes, transcendentals=0
        ),
        name="pack",
    )(target, counts, inner)


def share_kernel(mine_ref, *refs):
    tiles, shares_ref = refs[:-1], refs[-1]
    values = [mine_ref[0].astype(jnp.float32)]
    for ref in tiles:
        tile = ref[...].astype(jnp.float32)
        values.append(tile[0, 0] * 256.0 + tile[1, 0])
    total = values[0]
    for value in values[1:]:
        total = total + value
    for g, value in enumerate(values):
        shares_ref[g] = value / total


def share(counts, arrived):
    scalar = pl.BlockSpec(memory_space=pltpu.SMEM)
    last = arrived[0].shape[0] // spare - 1
    tile = pl.BlockSpec((spare, lanes), lambda i: (last, 0))
    return pl.pallas_call(
        share_kernel,
        grid=(1,),
        in_specs=[scalar] + [tile] * len(arrived),
        out_specs=scalar,
        out_shape=jax.ShapeDtypeStruct((1 + len(arrived),), jnp.float32),
        name="share",
    )(counts, *arrived)


def update_kernel(groups, me_ref, shares_ref, anchor_ref, inner_ref, *refs):
    arrived, momentum_ref = refs[: groups - 1], refs[groups - 1]
    new_ref, weights_ref, moments_ref = refs[-3:]
    base = anchor_ref[...].astype(jnp.float32)
    pseudo = shares_ref[0] * (base - inner_ref[...].astype(jnp.float32))
    for g, block_ref in enumerate(arrived, 1):
        block = block_ref[...].astype(jnp.float32).reshape(base.shape)
        pseudo = pseudo + shares_ref[g] * (base - block)
    moment = momentum_rate * momentum_ref[...] + pseudo
    new = (base - outer_rate * (pseudo + momentum_rate * moment)).astype(jnp.bfloat16)
    moments_ref[...] = moment
    weights_ref[...] = new
    new_ref[...] = new


def update(groups, chunk, me, shares, anchor, inner, arrived, momentum, held):
    _, owned, width = momentum.shape
    lo, row, rows = chunk.lo, chunk.row, chunk.rows
    if arrived[0].ndim == 2:
        grid = (1, width // lanes)
        block = (1, rows, lanes)
        ahead, mine = row // rows, owned // rows
        came = pl.BlockSpec((rows, lanes), lambda p, j, me_ref: (j, 0))
        packed = pl.BlockSpec(block, lambda p, j, me_ref: (0, 0, j))
        spread = pl.BlockSpec(block, lambda p, j, me_ref: (lo, me_ref[0] * mine + ahead, j))
        kept = pl.BlockSpec(block, lambda p, j, me_ref: (lo, ahead, j))
    else:
        tall = math.gcd(row, rows, owned, 128)
        grid = (chunk.parts, rows // tall)
        block = (1, tall, width)
        ahead, mine = row // tall, owned // tall
        came = pl.BlockSpec(block, lambda p, r, me_ref: (p, r, 0))
        packed = came
        spread = pl.BlockSpec(
            block, lambda p, r, me_ref: (lo + p, me_ref[0] * mine + ahead + r, 0)
        )
        kept = pl.BlockSpec(block, lambda p, r, me_ref: (lo + p, ahead + r, 0))
    scalar = pl.BlockSpec(memory_space=pltpu.SMEM)
    aliases = {groups + 4: 1, groups + 5: 2} if held else {}
    size = chunk.parts * rows * width
    return pl.pallas_call(
        functools.partial(update_kernel, groups),
        grid_spec=pltpu.PrefetchScalarGridSpec(
            num_scalar_prefetch=1,
            grid=grid,
            in_specs=[scalar, spread, spread]
            + [came] * (groups - 1)
            + [kept]
            + [pl.BlockSpec(memory_space=pl.ANY)] * len(held),
            out_specs=[packed, spread, kept],
        ),
        out_shape=[
            jax.ShapeDtypeStruct((chunk.parts, rows, width), jnp.bfloat16),
            jax.ShapeDtypeStruct(anchor.shape, jnp.bfloat16),
            jax.ShapeDtypeStruct(momentum.shape, jnp.float32),
        ],
        input_output_aliases=aliases,
        compiler_params=pltpu.CompilerParams(vmem_limit_bytes=vmem_bytes),
        cost_estimate=pl.CostEstimate(
            flops=12 * size, bytes_accessed=(14 + 2 * groups) * size, transcendentals=0
        ),
        name="update",
    )(me, shares, anchor, inner, *arrived, momentum, *held)


def place_kernel(owned, chunk, at_ref, block_ref, _, weights_ref, sem):
    start = pl.multiple_of(at_ref[0] * owned + chunk.row, spare)
    copy = pltpu.make_async_copy(
        block_ref, weights_ref.at[pl.ds(chunk.lo, chunk.parts), pl.ds(start, chunk.rows), :], sem
    )
    copy.start()
    copy.wait()


def place(owned, chunk, at, block, weights):
    anywhere = pl.BlockSpec(memory_space=pl.ANY)
    return pl.pallas_call(
        functools.partial(place_kernel, owned, chunk),
        in_specs=[pl.BlockSpec(memory_space=pltpu.SMEM), anywhere, anywhere],
        out_specs=anywhere,
        out_shape=jax.ShapeDtypeStruct(weights.shape, weights.dtype),
        scratch_shapes=[pltpu.SemaphoreType.DMA],
        input_output_aliases={2: 0},
        compiler_params=pltpu.CompilerParams(vmem_limit_bytes=vmem_bytes),
        cost_estimate=pl.CostEstimate(flops=0, bytes_accessed=4 * block.size, transcendentals=0),
        name="place",
    )(at, block, weights)


def solution(mesh):
    groups = mesh.shape["replica"]

    def shifted(value, shift):
        pairs = [(i, (i + shift) % groups) for i in range(groups)]
        return lax.ppermute(value, "replica", pairs)

    def on_device(counts, inner, anchor, momentum):
        shape = anchor.shape
        owned, width = momentum.shape[-2:]
        parts = shape[0] * shape[1]
        inner = inner.reshape(parts, *shape[-2:])
        anchor = anchor.reshape(parts, *shape[-2:])
        momentum = momentum.reshape(parts, owned, width)
        me = lax.axis_index("replica")
        half = owned // 2
        last = max(16, owned // 8)
        chunks = [Chunk(0, 1, 0, half), Chunk(0, 1, half, half)]
        chunks += [Chunk(p, 1, 0, owned) for p in range(1, parts - 1)]
        chunks += [
            Chunk(parts - 1, 1, 0, owned - last),
            Chunk(parts - 1, 1, owned - last, last),
        ]
        shifts = range(1, groups)

        def rows_for(array, chunk, target):
            sizes = (chunk.parts, chunk.rows, width)
            return lax.dynamic_slice(array, (chunk.lo, target * owned + chunk.row, 0), sizes)

        targets = [(me + s) % groups for s in shifts]
        first = [rows_for(inner, chunks[0], t) for t in targets]
        first, rest, later_counts = lax.optimization_barrier((first, inner, counts))
        second = [
            pack(chunks[1], t.reshape(1).astype(jnp.int32), later_counts, rest, owned)
            for t in targets
        ]
        sent = [first, second] + [[rows_for(rest, c, t) for t in targets] for c in chunks[2:]]
        arrived = [[shifted(v, s) for v, s in zip(values, shifts)] for values in sent]
        shares = share(later_counts, arrived[1])

        where = me.reshape(1).astype(jnp.int32)
        held = []
        travelled = []
        for chunk, blocks in zip(chunks, arrived):
            new, *held = update(
                groups, chunk, where, shares, anchor, inner, blocks, momentum, held
            )
            travelled.append([shifted(new, s) for s in shifts])
        weights, moments = held
        for chunk, blocks in zip(chunks, travelled):
            for s, block in zip(shifts, blocks):
                source = ((me - s) % groups).reshape(1).astype(jnp.int32)
                weights = place(owned, chunk, source, block, weights)
        return weights.reshape(shape), moments.reshape(*shape[:2], owned, width)

    placed = (
        P("replica"),
        P("replica", None, None, "fsdp", None),
        P(None, None, "fsdp", None),
        P(None, None, ("fsdp", "replica"), None),
    )
    return jax.shard_map(
        on_device,
        mesh=mesh,
        in_specs=placed,
        out_specs=(P(None, None, "fsdp", None), P(None, None, ("fsdp", "replica"), None)),
        check_vma=False,
    )
```

```python
import functools
import math
from typing import NamedTuple

import jax
import jax.numpy as jnp
from jax import lax
from jax.experimental import pallas as pl
from jax.experimental.pallas import tpu as pltpu
from jax.sharding import PartitionSpec as P

outer_rate = 0.7
momentum_rate = 0.9
lanes = 128
spare = 16
vmem_bytes = 48 * 1024 * 1024


class Chunk(NamedTuple):
    lo: int
    parts: int
    row: int
    rows: int


def cut_kernel(groups, owned, chunk, shift, inner_ref, out_ref, sem):
    target = lax.rem(lax.axis_index("replica") + shift, groups)
    start = pl.multiple_of(target * owned + chunk.row, spare)
    copy = pltpu.make_async_copy(
        inner_ref.at[pl.ds(chunk.lo, chunk.parts), pl.ds(start, chunk.rows), :], out_ref, sem
    )
    copy.start()
    copy.wait()


def cut(groups, owned, chunk, shift, inner):
    shape = (chunk.parts, chunk.rows, inner.shape[2])
    return pl.pallas_call(
        functools.partial(cut_kernel, groups, owned, chunk, shift),
        in_specs=[pl.BlockSpec(memory_space=pl.ANY)],
        out_specs=pl.BlockSpec(memory_space=pltpu.VMEM),
        out_shape=jax.ShapeDtypeStruct(shape, inner.dtype),
        scratch_shapes=[pltpu.SemaphoreType.DMA],
        compiler_params=pltpu.CompilerParams(vmem_limit_bytes=vmem_bytes),
        cost_estimate=pl.CostEstimate(
            flops=0, bytes_accessed=4 * math.prod(shape), transcendentals=0
        ),
        name="cut",
    )(inner)


def pack_kernel(owned, part, row, target_ref, count_ref, inner_ref, out_ref, tile_ref, sems):
    rows = (out_ref.shape[0] - spare) // (inner_ref.shape[2] // lanes)
    start = pl.multiple_of(target_ref[0] * owned + row, spare)
    copies = [
        pltpu.make_async_copy(
            inner_ref.at[part, pl.ds(start, rows), pl.ds(j * lanes, lanes)],
            out_ref.at[pl.ds(j * rows, rows), :],
            sems.at[j],
        )
        for j in range(inner_ref.shape[2] // lanes)
    ]
    for copy in copies:
        copy.start()
    count = count_ref[0]
    high = (count >> 8).astype(jnp.float32)
    low = (count & 255).astype(jnp.float32)
    row = lax.broadcasted_iota(jnp.int32, tile_ref.shape, 0)
    tile_ref[...] = jnp.where(row == 0, high, low).astype(jnp.bfloat16)
    copies.append(
        pltpu.make_async_copy(
            tile_ref,
            out_ref.at[pl.ds(out_ref.shape[0] - spare, spare), :],
            sems.at[len(copies)],
        )
    )
    copies[-1].start()
    for copy in copies:
        copy.wait()


def pack(chunk, target, counts, inner, owned):
    part, row, rows = chunk.lo, chunk.row, chunk.rows
    blocks = inner.shape[2] // lanes
    scalar = pl.BlockSpec(memory_space=pltpu.SMEM)
    anywhere = pl.BlockSpec(memory_space=pl.ANY)
    return pl.pallas_call(
        functools.partial(pack_kernel, owned, part, row),
        in_specs=[scalar, scalar, anywhere],
        out_specs=anywhere,
        out_shape=jax.ShapeDtypeStruct((blocks * rows + spare, lanes), jnp.bfloat16),
        scratch_shapes=[
            pltpu.VMEM((spare, lanes), jnp.bfloat16),
            pltpu.SemaphoreType.DMA((blocks + 1,)),
        ],
        compiler_params=pltpu.CompilerParams(vmem_limit_bytes=vmem_bytes),
        cost_estimate=pl.CostEstimate(
            flops=0, bytes_accessed=4 * blocks * rows * lanes, transcendentals=0
        ),
        name="pack",
    )(target, counts, inner)


def share_kernel(mine_ref, *refs):
    tiles, shares_ref = refs[:-1], refs[-1]
    values = [mine_ref[0].astype(jnp.float32)]
    for ref in tiles:
        tile = ref[...].astype(jnp.float32)
        values.append(tile[0, 0] * 256.0 + tile[1, 0])
    total = values[0]
    for value in values[1:]:
        total = total + value
    for g, value in enumerate(values):
        shares_ref[g] = value / total


def share(counts, arrived):
    scalar = pl.BlockSpec(memory_space=pltpu.SMEM)
    last = arrived[0].shape[0] // spare - 1
    tile = pl.BlockSpec((spare, lanes), lambda i: (last, 0))
    return pl.pallas_call(
        share_kernel,
        grid=(1,),
        in_specs=[scalar] + [tile] * len(arrived),
        out_specs=scalar,
        out_shape=jax.ShapeDtypeStruct((1 + len(arrived),), jnp.float32),
        name="share",
    )(counts, *arrived)


def update_kernel(groups, me_ref, shares_ref, anchor_ref, inner_ref, *refs):
    arrived, momentum_ref = refs[: groups - 1], refs[groups - 1]
    new_ref, weights_ref, moments_ref = refs[-3:]
    base = anchor_ref[...].astype(jnp.float32)
    pseudo = shares_ref[0] * (base - inner_ref[...].astype(jnp.float32))
    for g, block_ref in enumerate(arrived, 1):
        block = block_ref[...].astype(jnp.float32).reshape(base.shape)
        pseudo = pseudo + shares_ref[g] * (base - block)
    moment = momentum_rate * momentum_ref[...] + pseudo
    new = (base - outer_rate * (pseudo + momentum_rate * moment)).astype(jnp.bfloat16)
    moments_ref[...] = moment
    weights_ref[...] = new
    new_ref[...] = new


def update(groups, chunk, me, shares, anchor, inner, arrived, momentum, held):
    _, owned, width = momentum.shape
    lo, row, rows = chunk.lo, chunk.row, chunk.rows
    if arrived[0].ndim == 2:
        grid = (1, width // lanes)
        block = (1, rows, lanes)
        ahead, mine = row // rows, owned // rows
        came = pl.BlockSpec((rows, lanes), lambda p, j, me_ref: (j, 0))
        packed = pl.BlockSpec(block, lambda p, j, me_ref: (0, 0, j))
        spread = pl.BlockSpec(block, lambda p, j, me_ref: (lo, me_ref[0] * mine + ahead, j))
        kept = pl.BlockSpec(block, lambda p, j, me_ref: (lo, ahead, j))
    else:
        tall = math.gcd(row, rows, owned, 128)
        grid = (chunk.parts, rows // tall)
        block = (1, tall, width)
        ahead, mine = row // tall, owned // tall
        came = pl.BlockSpec(block, lambda p, r, me_ref: (p, r, 0))
        packed = came
        spread = pl.BlockSpec(
            block, lambda p, r, me_ref: (lo + p, me_ref[0] * mine + ahead + r, 0)
        )
        kept = pl.BlockSpec(block, lambda p, r, me_ref: (lo + p, ahead + r, 0))
    scalar = pl.BlockSpec(memory_space=pltpu.SMEM)
    aliases = {groups + 4: 1, groups + 5: 2} if held else {}
    size = chunk.parts * rows * width
    return pl.pallas_call(
        functools.partial(update_kernel, groups),
        grid_spec=pltpu.PrefetchScalarGridSpec(
            num_scalar_prefetch=1,
            grid=grid,
            in_specs=[scalar, spread, spread]
            + [came] * (groups - 1)
            + [kept]
            + [pl.BlockSpec(memory_space=pl.ANY)] * len(held),
            out_specs=[packed, spread, kept],
        ),
        out_shape=[
            jax.ShapeDtypeStruct((chunk.parts, rows, width), jnp.bfloat16),
            jax.ShapeDtypeStruct(anchor.shape, jnp.bfloat16),
            jax.ShapeDtypeStruct(momentum.shape, jnp.float32),
        ],
        input_output_aliases=aliases,
        compiler_params=pltpu.CompilerParams(vmem_limit_bytes=vmem_bytes),
        cost_estimate=pl.CostEstimate(
            flops=12 * size, bytes_accessed=(14 + 2 * groups) * size, transcendentals=0
        ),
        name="update",
    )(me, shares, anchor, inner, *arrived, momentum, *held)


def place_kernel(groups, owned, chunk, shift, block_ref, _, weights_ref, sem):
    source = lax.rem(lax.axis_index("replica") + groups - shift, groups)
    start = pl.multiple_of(source * owned + chunk.row, spare)
    copy = pltpu.make_async_copy(
        block_ref, weights_ref.at[pl.ds(chunk.lo, chunk.parts), pl.ds(start, chunk.rows), :], sem
    )
    copy.start()
    copy.wait()


def place(groups, owned, chunk, shift, block, weights):
    anywhere = pl.BlockSpec(memory_space=pl.ANY)
    return pl.pallas_call(
        functools.partial(place_kernel, groups, owned, chunk, shift),
        in_specs=[anywhere, anywhere],
        out_specs=anywhere,
        out_shape=jax.ShapeDtypeStruct(weights.shape, weights.dtype),
        scratch_shapes=[pltpu.SemaphoreType.DMA],
        input_output_aliases={1: 0},
        compiler_params=pltpu.CompilerParams(vmem_limit_bytes=vmem_bytes),
        cost_estimate=pl.CostEstimate(flops=0, bytes_accessed=4 * block.size, transcendentals=0),
        name="place",
    )(block, weights)


def solution(mesh):
    groups = mesh.shape["replica"]

    def shifted(value, shift):
        pairs = [(i, (i + shift) % groups) for i in range(groups)]
        return lax.ppermute(value, "replica", pairs)

    def on_device(counts, inner, anchor, momentum):
        shape = anchor.shape
        owned, width = momentum.shape[-2:]
        parts = shape[0] * shape[1]
        inner = inner.reshape(parts, *shape[-2:])
        anchor = anchor.reshape(parts, *shape[-2:])
        momentum = momentum.reshape(parts, owned, width)
        me = lax.axis_index("replica")
        half = owned // 2
        last = max(16, owned // 4)
        chunks = [Chunk(0, 1, 0, half), Chunk(0, 1, half, half)]
        chunks += [Chunk(p, 1, 0, owned) for p in range(1, parts - 1)]
        chunks += [
            Chunk(parts - 1, 1, 0, owned - last),
            Chunk(parts - 1, 1, owned - last, last),
        ]
        shifts = range(1, groups)

        def rows_for(array, chunk, target):
            sizes = (chunk.parts, chunk.rows, width)
            return lax.dynamic_slice(array, (chunk.lo, target * owned + chunk.row, 0), sizes)

        targets = [(me + s) % groups for s in shifts]
        first = [cut(groups, owned, chunks[0], s, inner) for s in shifts]
        first, rest, later_counts = lax.optimization_barrier((first, inner, counts))
        second = [
            pack(chunks[1], t.reshape(1).astype(jnp.int32), later_counts, rest, owned)
            for t in targets
        ]
        sent = [first, second] + [[rows_for(rest, c, t) for t in targets] for c in chunks[2:]]
        arrived = [[shifted(v, s) for v, s in zip(values, shifts)] for values in sent]
        shares = share(later_counts, arrived[1])

        where = me.reshape(1).astype(jnp.int32)
        held = []
        travelled = []
        for chunk, blocks in zip(chunks, arrived):
            new, *held = update(
                groups, chunk, where, shares, anchor, inner, blocks, momentum, held
            )
            travelled.append([shifted(new, s) for s in shifts])
        weights, moments = held
        for chunk, blocks in zip(chunks, travelled):
            for s, block in zip(shifts, blocks):
                weights = place(groups, owned, chunk, s, block, weights)
        return weights.reshape(shape), moments.reshape(*shape[:2], owned, width)

    placed = (
        P("replica"),
        P("replica", None, None, "fsdp", None),
        P(None, None, "fsdp", None),
        P(None, None, ("fsdp", "replica"), None),
    )
    return jax.shard_map(
        on_device,
        mesh=mesh,
        in_specs=placed,
        out_specs=(P(None, None, "fsdp", None), P(None, None, ("fsdp", "replica"), None)),
        check_vma=False,
    )
```

```python
import functools
import math
from typing import NamedTuple

import jax
import jax.numpy as jnp
from jax import lax
from jax.experimental import pallas as pl
from jax.experimental.pallas import tpu as pltpu
from jax.sharding import PartitionSpec as P

outer_rate = 0.7
momentum_rate = 0.9
lanes = 128
spare = 16
vmem_bytes = 48 * 1024 * 1024


class Chunk(NamedTuple):
    lo: int
    parts: int
    row: int
    rows: int


def cut_kernel(groups, owned, chunk, shift, inner_ref, out_ref, sem):
    target = lax.rem(lax.axis_index("replica") + shift, groups)
    start = pl.multiple_of(target * owned + chunk.row, spare)
    copy = pltpu.make_async_copy(
        inner_ref.at[pl.ds(chunk.lo, chunk.parts), pl.ds(start, chunk.rows), :], out_ref, sem
    )
    copy.start()
    copy.wait()


def cut(groups, owned, chunk, shift, inner):
    shape = (chunk.parts, chunk.rows, inner.shape[2])
    return pl.pallas_call(
        functools.partial(cut_kernel, groups, owned, chunk, shift),
        in_specs=[pl.BlockSpec(memory_space=pl.ANY)],
        out_specs=pl.BlockSpec(memory_space=pltpu.VMEM),
        out_shape=jax.ShapeDtypeStruct(shape, inner.dtype),
        scratch_shapes=[pltpu.SemaphoreType.DMA],
        compiler_params=pltpu.CompilerParams(vmem_limit_bytes=vmem_bytes),
        cost_estimate=pl.CostEstimate(
            flops=0, bytes_accessed=4 * math.prod(shape), transcendentals=0
        ),
        name="cut",
    )(inner)


def pack_kernel(owned, part, row, target_ref, count_ref, inner_ref, out_ref, tile_ref, sems):
    rows = (out_ref.shape[0] - spare) // (inner_ref.shape[2] // lanes)
    start = pl.multiple_of(target_ref[0] * owned + row, spare)
    copies = [
        pltpu.make_async_copy(
            inner_ref.at[part, pl.ds(start, rows), pl.ds(j * lanes, lanes)],
            out_ref.at[pl.ds(j * rows, rows), :],
            sems.at[j],
        )
        for j in range(inner_ref.shape[2] // lanes)
    ]
    for copy in copies:
        copy.start()
    count = count_ref[0]
    high = (count >> 8).astype(jnp.float32)
    low = (count & 255).astype(jnp.float32)
    row = lax.broadcasted_iota(jnp.int32, tile_ref.shape, 0)
    tile_ref[...] = jnp.where(row == 0, high, low).astype(jnp.bfloat16)
    copies.append(
        pltpu.make_async_copy(
            tile_ref,
            out_ref.at[pl.ds(out_ref.shape[0] - spare, spare), :],
            sems.at[len(copies)],
        )
    )
    copies[-1].start()
    for copy in copies:
        copy.wait()


def pack(chunk, target, counts, inner, owned):
    part, row, rows = chunk.lo, chunk.row, chunk.rows
    blocks = inner.shape[2] // lanes
    scalar = pl.BlockSpec(memory_space=pltpu.SMEM)
    anywhere = pl.BlockSpec(memory_space=pl.ANY)
    return pl.pallas_call(
        functools.partial(pack_kernel, owned, part, row),
        in_specs=[scalar, scalar, anywhere],
        out_specs=anywhere,
        out_shape=jax.ShapeDtypeStruct((blocks * rows + spare, lanes), jnp.bfloat16),
        scratch_shapes=[
            pltpu.VMEM((spare, lanes), jnp.bfloat16),
            pltpu.SemaphoreType.DMA((blocks + 1,)),
        ],
        compiler_params=pltpu.CompilerParams(vmem_limit_bytes=vmem_bytes),
        cost_estimate=pl.CostEstimate(
            flops=0, bytes_accessed=4 * blocks * rows * lanes, transcendentals=0
        ),
        name="pack",
    )(target, counts, inner)


def share_kernel(mine_ref, *refs):
    tiles, shares_ref = refs[:-1], refs[-1]
    values = [mine_ref[0].astype(jnp.float32)]
    for ref in tiles:
        tile = ref[...].astype(jnp.float32)
        values.append(tile[0, 0] * 256.0 + tile[1, 0])
    total = values[0]
    for value in values[1:]:
        total = total + value
    for g, value in enumerate(values):
        shares_ref[g] = value / total


def share(counts, arrived):
    scalar = pl.BlockSpec(memory_space=pltpu.SMEM)
    last = arrived[0].shape[0] // spare - 1
    tile = pl.BlockSpec((spare, lanes), lambda i: (last, 0))
    return pl.pallas_call(
        share_kernel,
        grid=(1,),
        in_specs=[scalar] + [tile] * len(arrived),
        out_specs=scalar,
        out_shape=jax.ShapeDtypeStruct((1 + len(arrived),), jnp.float32),
        name="share",
    )(counts, *arrived)


def update_kernel(groups, me_ref, shares_ref, anchor_ref, inner_ref, *refs):
    arrived, momentum_ref = refs[: groups - 1], refs[groups - 1]
    new_ref, weights_ref, moments_ref = refs[-3:]
    base = anchor_ref[...].astype(jnp.float32)
    pseudo = shares_ref[0] * (base - inner_ref[...].astype(jnp.float32))
    for g, block_ref in enumerate(arrived, 1):
        block = block_ref[...].astype(jnp.float32).reshape(base.shape)
        pseudo = pseudo + shares_ref[g] * (base - block)
    moment = momentum_rate * momentum_ref[...] + pseudo
    new = (base - outer_rate * (pseudo + momentum_rate * moment)).astype(jnp.bfloat16)
    moments_ref[...] = moment
    weights_ref[...] = new
    new_ref[...] = new


def update(groups, chunk, me, shares, anchor, inner, arrived, momentum, held):
    _, owned, width = momentum.shape
    lo, row, rows = chunk.lo, chunk.row, chunk.rows
    if arrived[0].ndim == 2:
        grid = (1, width // lanes)
        block = (1, rows, lanes)
        ahead, mine = row // rows, owned // rows
        came = pl.BlockSpec((rows, lanes), lambda p, j, me_ref: (j, 0))
        packed = pl.BlockSpec(block, lambda p, j, me_ref: (0, 0, j))
        spread = pl.BlockSpec(block, lambda p, j, me_ref: (lo, me_ref[0] * mine + ahead, j))
        kept = pl.BlockSpec(block, lambda p, j, me_ref: (lo, ahead, j))
    else:
        tall = math.gcd(row, rows, owned, 128)
        grid = (chunk.parts, rows // tall)
        block = (1, tall, width)
        ahead, mine = row // tall, owned // tall
        came = pl.BlockSpec(block, lambda p, r, me_ref: (p, r, 0))
        packed = came
        spread = pl.BlockSpec(
            block, lambda p, r, me_ref: (lo + p, me_ref[0] * mine + ahead + r, 0)
        )
        kept = pl.BlockSpec(block, lambda p, r, me_ref: (lo + p, ahead + r, 0))
    scalar = pl.BlockSpec(memory_space=pltpu.SMEM)
    aliases = {groups + 4: 1, groups + 5: 2} if held else {}
    size = chunk.parts * rows * width
    return pl.pallas_call(
        functools.partial(update_kernel, groups),
        grid_spec=pltpu.PrefetchScalarGridSpec(
            num_scalar_prefetch=1,
            grid=grid,
            in_specs=[scalar, spread, spread]
            + [came] * (groups - 1)
            + [kept]
            + [pl.BlockSpec(memory_space=pl.ANY)] * len(held),
            out_specs=[packed, spread, kept],
        ),
        out_shape=[
            jax.ShapeDtypeStruct((chunk.parts, rows, width), jnp.bfloat16),
            jax.ShapeDtypeStruct(anchor.shape, jnp.bfloat16),
            jax.ShapeDtypeStruct(momentum.shape, jnp.float32),
        ],
        input_output_aliases=aliases,
        compiler_params=pltpu.CompilerParams(vmem_limit_bytes=vmem_bytes),
        cost_estimate=pl.CostEstimate(
            flops=12 * size, bytes_accessed=(14 + 2 * groups) * size, transcendentals=0
        ),
        name="update",
    )(me, shares, anchor, inner, *arrived, momentum, *held)


def place_kernel(groups, owned, chunk, shift, block_ref, _, weights_ref, sem):
    source = lax.rem(lax.axis_index("replica") + groups - shift, groups)
    start = pl.multiple_of(source * owned + chunk.row, spare)
    copy = pltpu.make_async_copy(
        block_ref, weights_ref.at[pl.ds(chunk.lo, chunk.parts), pl.ds(start, chunk.rows), :], sem
    )
    copy.start()
    copy.wait()


def place(groups, owned, chunk, shift, block, weights):
    anywhere = pl.BlockSpec(memory_space=pl.ANY)
    return pl.pallas_call(
        functools.partial(place_kernel, groups, owned, chunk, shift),
        in_specs=[anywhere, anywhere],
        out_specs=anywhere,
        out_shape=jax.ShapeDtypeStruct(weights.shape, weights.dtype),
        scratch_shapes=[pltpu.SemaphoreType.DMA],
        input_output_aliases={1: 0},
        compiler_params=pltpu.CompilerParams(vmem_limit_bytes=vmem_bytes),
        cost_estimate=pl.CostEstimate(flops=0, bytes_accessed=4 * block.size, transcendentals=0),
        name="place",
    )(block, weights)


def solution(mesh):
    groups = mesh.shape["replica"]

    def shifted(value, shift):
        pairs = [(i, (i + shift) % groups) for i in range(groups)]
        return lax.ppermute(value, "replica", pairs)

    def on_device(counts, inner, anchor, momentum):
        shape = anchor.shape
        owned, width = momentum.shape[-2:]
        parts = shape[0] * shape[1]
        inner = inner.reshape(parts, *shape[-2:])
        anchor = anchor.reshape(parts, *shape[-2:])
        momentum = momentum.reshape(parts, owned, width)
        me = lax.axis_index("replica")
        middle = (parts - 2) // 2
        chunks = [
            Chunk(1, middle, 0, owned),
            Chunk(1 + middle, parts - 2 - middle, 0, owned),
            Chunk(0, 1, 0, owned),
            Chunk(parts - 1, 1, 0, owned),
        ]
        shifts = range(1, groups)

        def rows_for(array, chunk, target):
            sizes = (chunk.parts, chunk.rows, width)
            return lax.dynamic_slice(array, (chunk.lo, target * owned + chunk.row, 0), sizes)

        targets = [(me + s) % groups for s in shifts]
        first = [cut(groups, owned, chunks[0], s, inner) for s in shifts]
        first, rest, later_counts = lax.optimization_barrier((first, inner, counts))
        sent = [first] + [[rows_for(rest, c, t) for t in targets] for c in chunks[1:]]
        sent[2] = [
            pack(chunks[2], t.reshape(1).astype(jnp.int32), later_counts, rest, owned)
            for t in targets
        ]
        arrived = [[shifted(v, s) for v, s in zip(values, shifts)] for values in sent]
        shares = share(later_counts, arrived[2])

        where = me.reshape(1).astype(jnp.int32)
        held = []
        travelled = []
        for chunk, blocks in zip(chunks, arrived):
            new, *held = update(
                groups, chunk, where, shares, anchor, inner, blocks, momentum, held
            )
            travelled.append([shifted(new, s) for s in shifts])
        weights, moments = held
        for chunk, blocks in zip(chunks, travelled):
            for s, block in zip(shifts, blocks):
                weights = place(groups, owned, chunk, s, block, weights)
        return weights.reshape(shape), moments.reshape(*shape[:2], owned, width)

    placed = (
        P("replica"),
        P("replica", None, None, "fsdp", None),
        P(None, None, "fsdp", None),
        P(None, None, ("fsdp", "replica"), None),
    )
    return jax.shard_map(
        on_device,
        mesh=mesh,
        in_specs=placed,
        out_specs=(P(None, None, "fsdp", None), P(None, None, ("fsdp", "replica"), None)),
        check_vma=False,
    )
```

```python
import functools
import math
from typing import NamedTuple

import jax
import jax.numpy as jnp
from jax import lax
from jax.experimental import pallas as pl
from jax.experimental.pallas import tpu as pltpu
from jax.sharding import PartitionSpec as P

outer_rate = 0.7
momentum_rate = 0.9
lanes = 128
spare = 16
vmem_bytes = 48 * 1024 * 1024


class Chunk(NamedTuple):
    lo: int
    parts: int
    row: int
    rows: int


def cut_kernel(groups, owned, chunk, shift, inner_ref, out_ref, sem):
    target = lax.rem(lax.axis_index("replica") + shift, groups)
    start = pl.multiple_of(target * owned + chunk.row, spare)
    copy = pltpu.make_async_copy(
        inner_ref.at[pl.ds(chunk.lo, chunk.parts), pl.ds(start, chunk.rows), :], out_ref, sem
    )
    copy.start()
    copy.wait()


def cut(groups, owned, chunk, shift, inner):
    shape = (chunk.parts, chunk.rows, inner.shape[2])
    return pl.pallas_call(
        functools.partial(cut_kernel, groups, owned, chunk, shift),
        in_specs=[pl.BlockSpec(memory_space=pl.ANY)],
        out_specs=pl.BlockSpec(memory_space=pltpu.VMEM),
        out_shape=jax.ShapeDtypeStruct(shape, inner.dtype),
        scratch_shapes=[pltpu.SemaphoreType.DMA],
        compiler_params=pltpu.CompilerParams(vmem_limit_bytes=vmem_bytes),
        cost_estimate=pl.CostEstimate(
            flops=0, bytes_accessed=4 * math.prod(shape), transcendentals=0
        ),
        name="cut",
    )(inner)


def pack_kernel(owned, part, row, target_ref, count_ref, inner_ref, out_ref, tile_ref, sems):
    rows = (out_ref.shape[0] - spare) // (inner_ref.shape[2] // lanes)
    start = pl.multiple_of(target_ref[0] * owned + row, spare)
    copies = [
        pltpu.make_async_copy(
            inner_ref.at[part, pl.ds(start, rows), pl.ds(j * lanes, lanes)],
            out_ref.at[pl.ds(j * rows, rows), :],
            sems.at[j],
        )
        for j in range(inner_ref.shape[2] // lanes)
    ]
    for copy in copies:
        copy.start()
    count = count_ref[0]
    high = (count >> 8).astype(jnp.float32)
    low = (count & 255).astype(jnp.float32)
    row = lax.broadcasted_iota(jnp.int32, tile_ref.shape, 0)
    tile_ref[...] = jnp.where(row == 0, high, low).astype(jnp.bfloat16)
    copies.append(
        pltpu.make_async_copy(
            tile_ref,
            out_ref.at[pl.ds(out_ref.shape[0] - spare, spare), :],
            sems.at[len(copies)],
        )
    )
    copies[-1].start()
    for copy in copies:
        copy.wait()


def pack(chunk, target, counts, inner, owned):
    part, row, rows = chunk.lo, chunk.row, chunk.rows
    blocks = inner.shape[2] // lanes
    scalar = pl.BlockSpec(memory_space=pltpu.SMEM)
    anywhere = pl.BlockSpec(memory_space=pl.ANY)
    return pl.pallas_call(
        functools.partial(pack_kernel, owned, part, row),
        in_specs=[scalar, scalar, anywhere],
        out_specs=anywhere,
        out_shape=jax.ShapeDtypeStruct((blocks * rows + spare, lanes), jnp.bfloat16),
        scratch_shapes=[
            pltpu.VMEM((spare, lanes), jnp.bfloat16),
            pltpu.SemaphoreType.DMA((blocks + 1,)),
        ],
        compiler_params=pltpu.CompilerParams(vmem_limit_bytes=vmem_bytes),
        cost_estimate=pl.CostEstimate(
            flops=0, bytes_accessed=4 * blocks * rows * lanes, transcendentals=0
        ),
        name="pack",
    )(target, counts, inner)


def share_kernel(mine_ref, *refs):
    tiles, shares_ref = refs[:-1], refs[-1]
    values = [mine_ref[0].astype(jnp.float32)]
    for ref in tiles:
        tile = ref[...].astype(jnp.float32)
        values.append(tile[0, 0] * 256.0 + tile[1, 0])
    total = values[0]
    for value in values[1:]:
        total = total + value
    for g, value in enumerate(values):
        shares_ref[g] = value / total


def share(counts, arrived):
    scalar = pl.BlockSpec(memory_space=pltpu.SMEM)
    last = arrived[0].shape[0] // spare - 1
    tile = pl.BlockSpec((spare, lanes), lambda i: (last, 0))
    return pl.pallas_call(
        share_kernel,
        grid=(1,),
        in_specs=[scalar] + [tile] * len(arrived),
        out_specs=scalar,
        out_shape=jax.ShapeDtypeStruct((1 + len(arrived),), jnp.float32),
        name="share",
    )(counts, *arrived)


def update_kernel(groups, me_ref, shares_ref, anchor_ref, inner_ref, *refs):
    arrived, momentum_ref = refs[: groups - 1], refs[groups - 1]
    new_ref, weights_ref, moments_ref = refs[-3:]
    base = anchor_ref[...].astype(jnp.float32)
    pseudo = shares_ref[0] * (base - inner_ref[...].astype(jnp.float32))
    for g, block_ref in enumerate(arrived, 1):
        block = block_ref[...].astype(jnp.float32).reshape(base.shape)
        pseudo = pseudo + shares_ref[g] * (base - block)
    moment = momentum_rate * momentum_ref[...] + pseudo
    new = (base - outer_rate * (pseudo + momentum_rate * moment)).astype(jnp.bfloat16)
    moments_ref[...] = moment
    weights_ref[...] = new
    new_ref[...] = new


def update(groups, chunk, me, shares, anchor, inner, arrived, momentum, held):
    _, owned, width = momentum.shape
    lo, row, rows = chunk.lo, chunk.row, chunk.rows
    if arrived[0].ndim == 2:
        grid = (1, width // lanes)
        block = (1, rows, lanes)
        ahead, mine = row // rows, owned // rows
        came = pl.BlockSpec((rows, lanes), lambda p, j, me_ref: (j, 0))
        packed = pl.BlockSpec(block, lambda p, j, me_ref: (0, 0, j))
        spread = pl.BlockSpec(block, lambda p, j, me_ref: (lo, me_ref[0] * mine + ahead, j))
        kept = pl.BlockSpec(block, lambda p, j, me_ref: (lo, ahead, j))
    else:
        tall = math.gcd(row, rows, owned, 128)
        grid = (chunk.parts, rows // tall)
        block = (1, tall, width)
        ahead, mine = row // tall, owned // tall
        came = pl.BlockSpec(block, lambda p, r, me_ref: (p, r, 0))
        packed = came
        spread = pl.BlockSpec(
            block, lambda p, r, me_ref: (lo + p, me_ref[0] * mine + ahead + r, 0)
        )
        kept = pl.BlockSpec(block, lambda p, r, me_ref: (lo + p, ahead + r, 0))
    scalar = pl.BlockSpec(memory_space=pltpu.SMEM)
    aliases = {groups + 4: 1, groups + 5: 2} if held else {}
    size = chunk.parts * rows * width
    return pl.pallas_call(
        functools.partial(update_kernel, groups),
        grid_spec=pltpu.PrefetchScalarGridSpec(
            num_scalar_prefetch=1,
            grid=grid,
            in_specs=[scalar, spread, spread]
            + [came] * (groups - 1)
            + [kept]
            + [pl.BlockSpec(memory_space=pl.ANY)] * len(held),
            out_specs=[packed, spread, kept],
        ),
        out_shape=[
            jax.ShapeDtypeStruct((chunk.parts, rows, width), jnp.bfloat16),
            jax.ShapeDtypeStruct(anchor.shape, jnp.bfloat16),
            jax.ShapeDtypeStruct(momentum.shape, jnp.float32),
        ],
        input_output_aliases=aliases,
        compiler_params=pltpu.CompilerParams(vmem_limit_bytes=vmem_bytes),
        cost_estimate=pl.CostEstimate(
            flops=12 * size, bytes_accessed=(14 + 2 * groups) * size, transcendentals=0
        ),
        name="update",
    )(me, shares, anchor, inner, *arrived, momentum, *held)


def solution(mesh):
    groups = mesh.shape["replica"]

    def shifted(value, shift):
        pairs = [(i, (i + shift) % groups) for i in range(groups)]
        return lax.ppermute(value, "replica", pairs)

    def on_device(counts, inner, anchor, momentum):
        shape = anchor.shape
        owned, width = momentum.shape[-2:]
        parts = shape[0] * shape[1]
        inner = inner.reshape(parts, *shape[-2:])
        anchor = anchor.reshape(parts, *shape[-2:])
        momentum = momentum.reshape(parts, owned, width)
        me = lax.axis_index("replica")
        half = owned // 2
        last = max(16, owned // 4)
        chunks = [Chunk(0, 1, 0, half), Chunk(0, 1, half, half)]
        chunks += [Chunk(p, 1, 0, owned) for p in range(1, parts - 1)]
        chunks += [
            Chunk(parts - 1, 1, 0, owned - last),
            Chunk(parts - 1, 1, owned - last, last),
        ]
        shifts = range(1, groups)

        def rows_for(array, chunk, target):
            sizes = (chunk.parts, chunk.rows, width)
            return lax.dynamic_slice(array, (chunk.lo, target * owned + chunk.row, 0), sizes)

        targets = [(me + s) % groups for s in shifts]
        first = [cut(groups, owned, chunks[0], s, inner) for s in shifts]
        first, rest, later_counts = lax.optimization_barrier((first, inner, counts))
        second = [
            pack(chunks[1], t.reshape(1).astype(jnp.int32), later_counts, rest, owned)
            for t in targets
        ]
        sent = [first, second] + [[rows_for(rest, c, t) for t in targets] for c in chunks[2:]]
        arrived = [[shifted(v, s) for v, s in zip(values, shifts)] for values in sent]
        shares = share(later_counts, arrived[1])

        where = me.reshape(1).astype(jnp.int32)
        held = []
        travelled = []
        for chunk, blocks in zip(chunks, arrived):
            new, *held = update(
                groups, chunk, where, shares, anchor, inner, blocks, momentum, held
            )
            travelled.append([shifted(new, s) for s in shifts])
        weights, moments = held
        for chunk, blocks in zip(chunks, travelled):
            for s, block in zip(shifts, blocks):
                source = (me - s) % groups
                weights = lax.dynamic_update_slice(
                    weights, block, (chunk.lo, source * owned + chunk.row, 0)
                )
        return weights.reshape(shape), moments.reshape(*shape[:2], owned, width)

    placed = (
        P("replica"),
        P("replica", None, None, "fsdp", None),
        P(None, None, "fsdp", None),
        P(None, None, ("fsdp", "replica"), None),
    )
    return jax.shard_map(
        on_device,
        mesh=mesh,
        in_specs=placed,
        out_specs=(P(None, None, "fsdp", None), P(None, None, ("fsdp", "replica"), None)),
        check_vma=False,
    )
```

```python
import functools
import math
from typing import NamedTuple

import jax
import jax.numpy as jnp
from jax import lax
from jax.experimental import pallas as pl
from jax.experimental.pallas import tpu as pltpu
from jax.sharding import PartitionSpec as P

outer_rate = 0.7
momentum_rate = 0.9
spare = 16
vmem_bytes = 48 * 1024 * 1024


class Chunk(NamedTuple):
    lo: int
    parts: int
    row: int
    rows: int


def cut_kernel(groups, owned, chunk, shift, inner_ref, out_ref, sem):
    target = lax.rem(lax.axis_index("replica") + shift, groups)
    start = pl.multiple_of(target * owned + chunk.row, spare)
    copy = pltpu.make_async_copy(
        inner_ref.at[pl.ds(chunk.lo, chunk.parts), pl.ds(start, chunk.rows), :], out_ref, sem
    )
    copy.start()
    copy.wait()


def cut(groups, owned, chunk, shift, inner):
    shape = (chunk.parts, chunk.rows, inner.shape[2])
    return pl.pallas_call(
        functools.partial(cut_kernel, groups, owned, chunk, shift),
        in_specs=[pl.BlockSpec(memory_space=pl.ANY)],
        out_specs=pl.BlockSpec(memory_space=pltpu.VMEM),
        out_shape=jax.ShapeDtypeStruct(shape, inner.dtype),
        scratch_shapes=[pltpu.SemaphoreType.DMA],
        compiler_params=pltpu.CompilerParams(vmem_limit_bytes=vmem_bytes),
        cost_estimate=pl.CostEstimate(
            flops=0, bytes_accessed=4 * math.prod(shape), transcendentals=0
        ),
        name="cut",
    )(inner)


def share_kernel(*refs):
    counts, shares_ref = refs[:-1], refs[-1]
    values = [ref[0].astype(jnp.float32) for ref in counts]
    total = values[0]
    for value in values[1:]:
        total = total + value
    for g, value in enumerate(values):
        shares_ref[g] = value / total


def share(counts):
    scalar = pl.BlockSpec(memory_space=pltpu.SMEM)
    return pl.pallas_call(
        share_kernel,
        in_specs=[scalar] * len(counts),
        out_specs=scalar,
        out_shape=jax.ShapeDtypeStruct((len(counts),), jnp.float32),
        name="share",
    )(*counts)


def update_kernel(groups, me_ref, shares_ref, anchor_ref, inner_ref, *refs):
    arrived, momentum_ref = refs[: groups - 1], refs[groups - 1]
    new_ref, weights_ref, moments_ref = refs[-3:]
    base = anchor_ref[...].astype(jnp.float32)
    pseudo = shares_ref[0] * (base - inner_ref[...].astype(jnp.float32))
    for g, block_ref in enumerate(arrived, 1):
        pseudo = pseudo + shares_ref[g] * (base - block_ref[...].astype(jnp.float32))
    moment = momentum_rate * momentum_ref[...] + pseudo
    new = (base - outer_rate * (pseudo + momentum_rate * moment)).astype(jnp.bfloat16)
    moments_ref[...] = moment
    weights_ref[...] = new
    new_ref[...] = new


def update(groups, chunk, me, shares, anchor, inner, arrived, momentum, held):
    _, owned, width = momentum.shape
    lo, row, rows = chunk.lo, chunk.row, chunk.rows
    tall = math.gcd(row, rows, owned, 128)
    grid = (chunk.parts, rows // tall)
    block = (1, tall, width)
    ahead, mine = row // tall, owned // tall
    came = pl.BlockSpec(block, lambda p, r, me_ref: (p, r, 0))
    packed = came
    spread = pl.BlockSpec(
        block, lambda p, r, me_ref: (lo + p, me_ref[0] * mine + ahead + r, 0)
    )
    kept = pl.BlockSpec(block, lambda p, r, me_ref: (lo + p, ahead + r, 0))
    scalar = pl.BlockSpec(memory_space=pltpu.SMEM)
    aliases = {groups + 4: 1, groups + 5: 2} if held else {}
    size = chunk.parts * rows * width
    return pl.pallas_call(
        functools.partial(update_kernel, groups),
        grid_spec=pltpu.PrefetchScalarGridSpec(
            num_scalar_prefetch=1,
            grid=grid,
            in_specs=[scalar, spread, spread]
            + [came] * (groups - 1)
            + [kept]
            + [pl.BlockSpec(memory_space=pl.ANY)] * len(held),
            out_specs=[packed, spread, kept],
        ),
        out_shape=[
            jax.ShapeDtypeStruct((chunk.parts, rows, width), jnp.bfloat16),
            jax.ShapeDtypeStruct(anchor.shape, jnp.bfloat16),
            jax.ShapeDtypeStruct(momentum.shape, jnp.float32),
        ],
        input_output_aliases=aliases,
        compiler_params=pltpu.CompilerParams(vmem_limit_bytes=vmem_bytes),
        cost_estimate=pl.CostEstimate(
            flops=12 * size, bytes_accessed=(14 + 2 * groups) * size, transcendentals=0
        ),
        name="update",
    )(me, shares, anchor, inner, *arrived, momentum, *held)


def place_kernel(groups, owned, chunk, shift, block_ref, _, weights_ref, sem):
    source = lax.rem(lax.axis_index("replica") + groups - shift, groups)
    start = pl.multiple_of(source * owned + chunk.row, spare)
    copy = pltpu.make_async_copy(
        block_ref, weights_ref.at[pl.ds(chunk.lo, chunk.parts), pl.ds(start, chunk.rows), :], sem
    )
    copy.start()
    copy.wait()


def place(groups, owned, chunk, shift, block, weights):
    anywhere = pl.BlockSpec(memory_space=pl.ANY)
    return pl.pallas_call(
        functools.partial(place_kernel, groups, owned, chunk, shift),
        in_specs=[anywhere, anywhere],
        out_specs=anywhere,
        out_shape=jax.ShapeDtypeStruct(weights.shape, weights.dtype),
        scratch_shapes=[pltpu.SemaphoreType.DMA],
        input_output_aliases={1: 0},
        compiler_params=pltpu.CompilerParams(vmem_limit_bytes=vmem_bytes),
        cost_estimate=pl.CostEstimate(flops=0, bytes_accessed=4 * block.size, transcendentals=0),
        name="place",
    )(block, weights)


def solution(mesh):
    groups = mesh.shape["replica"]

    def shifted(value, shift):
        pairs = [(i, (i + shift) % groups) for i in range(groups)]
        return lax.ppermute(value, "replica", pairs)

    def on_device(counts, inner, anchor, momentum):
        shape = anchor.shape
        owned, width = momentum.shape[-2:]
        parts = shape[0] * shape[1]
        inner = inner.reshape(parts, *shape[-2:])
        anchor = anchor.reshape(parts, *shape[-2:])
        momentum = momentum.reshape(parts, owned, width)
        me = lax.axis_index("replica")
        middle = (parts - 2) // 2
        chunks = [
            Chunk(1, middle, 0, owned),
            Chunk(1 + middle, parts - 2 - middle, 0, owned),
            Chunk(0, 1, 0, owned),
            Chunk(parts - 1, 1, 0, owned),
        ]
        shifts = range(1, groups)

        def rows_for(array, chunk, target):
            sizes = (chunk.parts, chunk.rows, width)
            return lax.dynamic_slice(array, (chunk.lo, target * owned + chunk.row, 0), sizes)

        targets = [(me + s) % groups for s in shifts]
        first = [cut(groups, owned, chunks[0], s, inner) for s in shifts]
        first, rest, later_counts = lax.optimization_barrier((first, inner, counts))
        sent = [first] + [[rows_for(rest, c, t) for t in targets] for c in chunks[1:]]
        arrived = [[shifted(v, s) for v, s in zip(values, shifts)] for values in sent]
        shares = share([counts] + [shifted(later_counts, s) for s in shifts])

        where = me.reshape(1).astype(jnp.int32)
        held = []
        travelled = []
        for chunk, blocks in zip(chunks, arrived):
            new, *held = update(
                groups, chunk, where, shares, anchor, inner, blocks, momentum, held
            )
            travelled.append([shifted(new, s) for s in shifts])
        weights, moments = held
        for chunk, blocks in zip(chunks, travelled):
            for s, block in zip(shifts, blocks):
                weights = place(groups, owned, chunk, s, block, weights)
        return weights.reshape(shape), moments.reshape(*shape[:2], owned, width)

    placed = (
        P("replica"),
        P("replica", None, None, "fsdp", None),
        P(None, None, "fsdp", None),
        P(None, None, ("fsdp", "replica"), None),
    )
    return jax.shard_map(
        on_device,
        mesh=mesh,
        in_specs=placed,
        out_specs=(P(None, None, "fsdp", None), P(None, None, ("fsdp", "replica"), None)),
        check_vma=False,
    )
```

```python
import functools
import math
from typing import NamedTuple

import jax
import jax.numpy as jnp
from jax import lax
from jax.experimental import pallas as pl
from jax.experimental.pallas import tpu as pltpu
from jax.sharding import PartitionSpec as P

outer_rate = 0.7
momentum_rate = 0.9
spare = 16
vmem_bytes = 48 * 1024 * 1024


class Chunk(NamedTuple):
    lo: int
    parts: int
    row: int
    rows: int


def cut_kernel(groups, owned, chunk, shift, inner_ref, out_ref, sem):
    target = lax.rem(lax.axis_index("replica") + shift, groups)
    start = pl.multiple_of(target * owned + chunk.row, spare)
    copy = pltpu.make_async_copy(
        inner_ref.at[pl.ds(chunk.lo, chunk.parts), pl.ds(start, chunk.rows), :], out_ref, sem
    )
    copy.start()
    copy.wait()


def cut(groups, owned, chunk, shift, inner):
    shape = (chunk.parts, chunk.rows, inner.shape[2])
    return pl.pallas_call(
        functools.partial(cut_kernel, groups, owned, chunk, shift),
        in_specs=[pl.BlockSpec(memory_space=pl.ANY)],
        out_specs=pl.BlockSpec(memory_space=pltpu.VMEM),
        out_shape=jax.ShapeDtypeStruct(shape, inner.dtype),
        scratch_shapes=[pltpu.SemaphoreType.DMA],
        compiler_params=pltpu.CompilerParams(vmem_limit_bytes=vmem_bytes),
        cost_estimate=pl.CostEstimate(
            flops=0, bytes_accessed=4 * math.prod(shape), transcendentals=0
        ),
        name="cut",
    )(inner)


def share_kernel(*refs):
    counts, shares_ref = refs[:-1], refs[-1]
    values = [ref[0].astype(jnp.float32) for ref in counts]
    total = values[0]
    for value in values[1:]:
        total = total + value
    for g, value in enumerate(values):
        shares_ref[g] = value / total


def share(counts):
    scalar = pl.BlockSpec(memory_space=pltpu.SMEM)
    return pl.pallas_call(
        share_kernel,
        in_specs=[scalar] * len(counts),
        out_specs=scalar,
        out_shape=jax.ShapeDtypeStruct((len(counts),), jnp.float32),
        name="share",
    )(*counts)


def update_kernel(groups, me_ref, shares_ref, anchor_ref, inner_ref, *refs):
    arrived, momentum_ref = refs[: groups - 1], refs[groups - 1]
    new_ref, weights_ref, moments_ref = refs[-3:]
    base = anchor_ref[...].astype(jnp.float32)
    pseudo = shares_ref[0] * (base - inner_ref[...].astype(jnp.float32))
    for g, block_ref in enumerate(arrived, 1):
        pseudo = pseudo + shares_ref[g] * (base - block_ref[...].astype(jnp.float32))
    moment = momentum_rate * momentum_ref[...] + pseudo
    new = (base - outer_rate * (pseudo + momentum_rate * moment)).astype(jnp.bfloat16)
    moments_ref[...] = moment
    weights_ref[...] = new
    new_ref[...] = new


def update(groups, chunk, me, shares, anchor, inner, arrived, momentum, held):
    _, owned, width = momentum.shape
    lo, row, rows = chunk.lo, chunk.row, chunk.rows
    tall = math.gcd(row, rows, owned, 128)
    grid = (chunk.parts, rows // tall)
    block = (1, tall, width)
    ahead, mine = row // tall, owned // tall
    came = pl.BlockSpec(block, lambda p, r, me_ref: (p, r, 0))
    packed = came
    spread = pl.BlockSpec(
        block, lambda p, r, me_ref: (lo + p, me_ref[0] * mine + ahead + r, 0)
    )
    kept = pl.BlockSpec(block, lambda p, r, me_ref: (lo + p, ahead + r, 0))
    scalar = pl.BlockSpec(memory_space=pltpu.SMEM)
    aliases = {groups + 4: 1, groups + 5: 2} if held else {}
    size = chunk.parts * rows * width
    return pl.pallas_call(
        functools.partial(update_kernel, groups),
        grid_spec=pltpu.PrefetchScalarGridSpec(
            num_scalar_prefetch=1,
            grid=grid,
            in_specs=[scalar, spread, spread]
            + [came] * (groups - 1)
            + [kept]
            + [pl.BlockSpec(memory_space=pl.ANY)] * len(held),
            out_specs=[packed, spread, kept],
        ),
        out_shape=[
            jax.ShapeDtypeStruct((chunk.parts, rows, width), jnp.bfloat16),
            jax.ShapeDtypeStruct(anchor.shape, jnp.bfloat16),
            jax.ShapeDtypeStruct(momentum.shape, jnp.float32),
        ],
        input_output_aliases=aliases,
        compiler_params=pltpu.CompilerParams(vmem_limit_bytes=vmem_bytes),
        cost_estimate=pl.CostEstimate(
            flops=12 * size, bytes_accessed=(14 + 2 * groups) * size, transcendentals=0
        ),
        name="update",
    )(me, shares, anchor, inner, *arrived, momentum, *held)


def place_kernel(groups, owned, chunk, shift, block_ref, _, weights_ref, sem):
    source = lax.rem(lax.axis_index("replica") + groups - shift, groups)
    start = pl.multiple_of(source * owned + chunk.row, spare)
    copy = pltpu.make_async_copy(
        block_ref, weights_ref.at[pl.ds(chunk.lo, chunk.parts), pl.ds(start, chunk.rows), :], sem
    )
    copy.start()
    copy.wait()


def place(groups, owned, chunk, shift, block, weights):
    anywhere = pl.BlockSpec(memory_space=pl.ANY)
    return pl.pallas_call(
        functools.partial(place_kernel, groups, owned, chunk, shift),
        in_specs=[anywhere, anywhere],
        out_specs=anywhere,
        out_shape=jax.ShapeDtypeStruct(weights.shape, weights.dtype),
        scratch_shapes=[pltpu.SemaphoreType.DMA],
        input_output_aliases={1: 0},
        compiler_params=pltpu.CompilerParams(vmem_limit_bytes=vmem_bytes),
        cost_estimate=pl.CostEstimate(flops=0, bytes_accessed=4 * block.size, transcendentals=0),
        name="place",
    )(block, weights)


def solution(mesh):
    groups = mesh.shape["replica"]

    def shifted(value, shift):
        pairs = [(i, (i + shift) % groups) for i in range(groups)]
        return lax.ppermute(value, "replica", pairs)

    def on_device(counts, inner, anchor, momentum):
        shape = anchor.shape
        owned, width = momentum.shape[-2:]
        parts = shape[0] * shape[1]
        inner = inner.reshape(parts, *shape[-2:])
        anchor = anchor.reshape(parts, *shape[-2:])
        momentum = momentum.reshape(parts, owned, width)
        me = lax.axis_index("replica")
        last = max(16, owned // 4)
        top = owned - last
        chunks = [Chunk(0, parts - 1, top, last)]
        chunks += [Chunk(p, 1, 0, top) for p in range(parts)]
        chunks += [Chunk(parts - 1, 1, top, last)]
        shifts = range(1, groups)

        def rows_for(array, chunk, target):
            sizes = (chunk.parts, chunk.rows, width)
            return lax.dynamic_slice(array, (chunk.lo, target * owned + chunk.row, 0), sizes)

        targets = [(me + s) % groups for s in shifts]
        first = [cut(groups, owned, chunks[0], s, inner) for s in shifts]
        first, rest, later_counts = lax.optimization_barrier((first, inner, counts))
        sent = [first] + [[rows_for(rest, c, t) for t in targets] for c in chunks[1:]]
        arrived = [[shifted(v, s) for v, s in zip(values, shifts)] for values in sent]
        shares = share([counts] + [shifted(later_counts, s) for s in shifts])

        where = me.reshape(1).astype(jnp.int32)
        held = []
        travelled = []
        for chunk, blocks in zip(chunks, arrived):
            new, *held = update(
                groups, chunk, where, shares, anchor, inner, blocks, momentum, held
            )
            travelled.append([shifted(new, s) for s in shifts])
        weights, moments = held
        for chunk, blocks in zip(chunks, travelled):
            for s, block in zip(shifts, blocks):
                weights = place(groups, owned, chunk, s, block, weights)
        return weights.reshape(shape), moments.reshape(*shape[:2], owned, width)

    placed = (
        P("replica"),
        P("replica", None, None, "fsdp", None),
        P(None, None, "fsdp", None),
        P(None, None, ("fsdp", "replica"), None),
    )
    return jax.shard_map(
        on_device,
        mesh=mesh,
        in_specs=placed,
        out_specs=(P(None, None, "fsdp", None), P(None, None, ("fsdp", "replica"), None)),
        check_vma=False,
    )
```

```python
import functools
import math
from typing import NamedTuple

import jax
import jax.numpy as jnp
from jax import lax
from jax.experimental import pallas as pl
from jax.experimental.pallas import tpu as pltpu
from jax.sharding import PartitionSpec as P

outer_rate = 0.7
momentum_rate = 0.9
spare = 16
vmem_bytes = 48 * 1024 * 1024


class Chunk(NamedTuple):
    lo: int
    parts: int
    row: int
    rows: int


def cut_kernel(groups, owned, chunk, shift, inner_ref, out_ref, sems):
    target = lax.rem(lax.axis_index("replica") + shift, groups)
    start = pl.multiple_of(target * owned + chunk.row, spare)
    copies = [
        pltpu.make_async_copy(
            inner_ref.at[chunk.lo + p, pl.ds(start, chunk.rows), :], out_ref.at[p], sems.at[p]
        )
        for p in range(chunk.parts)
    ]
    for copy in copies:
        copy.start()
    for copy in copies:
        copy.wait()


def cut(groups, owned, chunk, shift, inner):
    shape = (chunk.parts, chunk.rows, inner.shape[2])
    return pl.pallas_call(
        functools.partial(cut_kernel, groups, owned, chunk, shift),
        in_specs=[pl.BlockSpec(memory_space=pl.ANY)],
        out_specs=pl.BlockSpec(memory_space=pltpu.VMEM),
        out_shape=jax.ShapeDtypeStruct(shape, inner.dtype),
        scratch_shapes=[pltpu.SemaphoreType.DMA((chunk.parts,))],
        compiler_params=pltpu.CompilerParams(vmem_limit_bytes=vmem_bytes),
        cost_estimate=pl.CostEstimate(
            flops=0, bytes_accessed=4 * math.prod(shape), transcendentals=0
        ),
        name="cut",
    )(inner)


def share_kernel(*refs):
    counts, shares_ref = refs[:-1], refs[-1]
    values = [ref[0].astype(jnp.float32) for ref in counts]
    total = values[0]
    for value in values[1:]:
        total = total + value
    for g, value in enumerate(values):
        shares_ref[g] = value / total


def share(counts):
    scalar = pl.BlockSpec(memory_space=pltpu.SMEM)
    return pl.pallas_call(
        share_kernel,
        in_specs=[scalar] * len(counts),
        out_specs=scalar,
        out_shape=jax.ShapeDtypeStruct((len(counts),), jnp.float32),
        name="share",
    )(*counts)


def update_kernel(groups, me_ref, shares_ref, anchor_ref, inner_ref, *refs):
    arrived, momentum_ref = refs[: groups - 1], refs[groups - 1]
    new_ref, weights_ref, moments_ref = refs[-3:]
    base = anchor_ref[...].astype(jnp.float32)
    pseudo = shares_ref[0] * (base - inner_ref[...].astype(jnp.float32))
    for g, block_ref in enumerate(arrived, 1):
        pseudo = pseudo + shares_ref[g] * (base - block_ref[...].astype(jnp.float32))
    moment = momentum_rate * momentum_ref[...] + pseudo
    new = (base - outer_rate * (pseudo + momentum_rate * moment)).astype(jnp.bfloat16)
    moments_ref[...] = moment
    weights_ref[...] = new
    new_ref[...] = new


def update(groups, chunk, me, shares, anchor, inner, arrived, momentum, held):
    _, owned, width = momentum.shape
    lo, row, rows = chunk.lo, chunk.row, chunk.rows
    tall = math.gcd(row, rows, owned, 128)
    grid = (chunk.parts, rows // tall)
    block = (1, tall, width)
    ahead, mine = row // tall, owned // tall
    came = pl.BlockSpec(block, lambda p, r, me_ref: (p, r, 0))
    packed = came
    spread = pl.BlockSpec(
        block, lambda p, r, me_ref: (lo + p, me_ref[0] * mine + ahead + r, 0)
    )
    kept = pl.BlockSpec(block, lambda p, r, me_ref: (lo + p, ahead + r, 0))
    scalar = pl.BlockSpec(memory_space=pltpu.SMEM)
    aliases = {groups + 4: 1, groups + 5: 2} if held else {}
    size = chunk.parts * rows * width
    return pl.pallas_call(
        functools.partial(update_kernel, groups),
        grid_spec=pltpu.PrefetchScalarGridSpec(
            num_scalar_prefetch=1,
            grid=grid,
            in_specs=[scalar, spread, spread]
            + [came] * (groups - 1)
            + [kept]
            + [pl.BlockSpec(memory_space=pl.ANY)] * len(held),
            out_specs=[packed, spread, kept],
        ),
        out_shape=[
            jax.ShapeDtypeStruct((chunk.parts, rows, width), jnp.bfloat16),
            jax.ShapeDtypeStruct(anchor.shape, jnp.bfloat16),
            jax.ShapeDtypeStruct(momentum.shape, jnp.float32),
        ],
        input_output_aliases=aliases,
        compiler_params=pltpu.CompilerParams(vmem_limit_bytes=vmem_bytes),
        cost_estimate=pl.CostEstimate(
            flops=12 * size, bytes_accessed=(14 + 2 * groups) * size, transcendentals=0
        ),
        name="update",
    )(me, shares, anchor, inner, *arrived, momentum, *held)


def place_kernel(groups, owned, chunk, shift, block_ref, _, weights_ref, sem):
    source = lax.rem(lax.axis_index("replica") + groups - shift, groups)
    start = pl.multiple_of(source * owned + chunk.row, spare)
    copy = pltpu.make_async_copy(
        block_ref, weights_ref.at[pl.ds(chunk.lo, chunk.parts), pl.ds(start, chunk.rows), :], sem
    )
    copy.start()
    copy.wait()


def place(groups, owned, chunk, shift, block, weights):
    anywhere = pl.BlockSpec(memory_space=pl.ANY)
    return pl.pallas_call(
        functools.partial(place_kernel, groups, owned, chunk, shift),
        in_specs=[anywhere, anywhere],
        out_specs=anywhere,
        out_shape=jax.ShapeDtypeStruct(weights.shape, weights.dtype),
        scratch_shapes=[pltpu.SemaphoreType.DMA],
        input_output_aliases={1: 0},
        compiler_params=pltpu.CompilerParams(vmem_limit_bytes=vmem_bytes),
        cost_estimate=pl.CostEstimate(flops=0, bytes_accessed=4 * block.size, transcendentals=0),
        name="place",
    )(block, weights)


def solution(mesh):
    groups = mesh.shape["replica"]

    def shifted(value, shift):
        pairs = [(i, (i + shift) % groups) for i in range(groups)]
        return lax.ppermute(value, "replica", pairs)

    def on_device(counts, inner, anchor, momentum):
        shape = anchor.shape
        owned, width = momentum.shape[-2:]
        parts = shape[0] * shape[1]
        inner = inner.reshape(parts, *shape[-2:])
        anchor = anchor.reshape(parts, *shape[-2:])
        momentum = momentum.reshape(parts, owned, width)
        me = lax.axis_index("replica")
        last = max(16, owned // 4)
        top = owned - last
        early = 2 * parts // 3
        chunks = [Chunk(0, early, top, last)]
        chunks += [Chunk(p, 1, 0, top) for p in range(parts)]
        chunks += [Chunk(early, parts - early, top, last)]
        shifts = range(1, groups)

        def rows_for(array, chunk, target):
            sizes = (chunk.parts, chunk.rows, width)
            return lax.dynamic_slice(array, (chunk.lo, target * owned + chunk.row, 0), sizes)

        targets = [(me + s) % groups for s in shifts]
        first = [cut(groups, owned, chunks[0], s, inner) for s in shifts]
        first, rest, later_counts = lax.optimization_barrier((first, inner, counts))
        sent = [first] + [[rows_for(rest, c, t) for t in targets] for c in chunks[1:]]
        arrived = [[shifted(v, s) for v, s in zip(values, shifts)] for values in sent]
        shares = share([counts] + [shifted(later_counts, s) for s in shifts])

        where = me.reshape(1).astype(jnp.int32)
        held = []
        travelled = []
        for chunk, blocks in zip(chunks, arrived):
            new, *held = update(
                groups, chunk, where, shares, anchor, inner, blocks, momentum, held
            )
            travelled.append([shifted(new, s) for s in shifts])
        weights, moments = held
        for chunk, blocks in zip(chunks, travelled):
            for s, block in zip(shifts, blocks):
                weights = place(groups, owned, chunk, s, block, weights)
        return weights.reshape(shape), moments.reshape(*shape[:2], owned, width)

    placed = (
        P("replica"),
        P("replica", None, None, "fsdp", None),
        P(None, None, "fsdp", None),
        P(None, None, ("fsdp", "replica"), None),
    )
    return jax.shard_map(
        on_device,
        mesh=mesh,
        in_specs=placed,
        out_specs=(P(None, None, "fsdp", None), P(None, None, ("fsdp", "replica"), None)),
        check_vma=False,
    )
```

```python
import functools
import math
from typing import NamedTuple

import jax
import jax.numpy as jnp
from jax import lax
from jax.experimental import pallas as pl
from jax.experimental.pallas import tpu as pltpu
from jax.sharding import PartitionSpec as P

outer_rate = 0.7
momentum_rate = 0.9
lanes = 128
spare = 16
vmem_bytes = 48 * 1024 * 1024


class Chunk(NamedTuple):
    lo: int
    parts: int
    row: int
    rows: int


def cut_kernel(groups, owned, chunk, shift, inner_ref, out_ref, sem):
    target = lax.rem(lax.axis_index("replica") + shift, groups)
    start = pl.multiple_of(target * owned + chunk.row, spare)
    copy = pltpu.make_async_copy(
        inner_ref.at[pl.ds(chunk.lo, chunk.parts), pl.ds(start, chunk.rows), :], out_ref, sem
    )
    copy.start()
    copy.wait()


def cut(groups, owned, chunk, shift, inner):
    shape = (chunk.parts, chunk.rows, inner.shape[2])
    return pl.pallas_call(
        functools.partial(cut_kernel, groups, owned, chunk, shift),
        in_specs=[pl.BlockSpec(memory_space=pl.ANY)],
        out_specs=pl.BlockSpec(memory_space=pltpu.VMEM),
        out_shape=jax.ShapeDtypeStruct(shape, inner.dtype),
        scratch_shapes=[pltpu.SemaphoreType.DMA],
        compiler_params=pltpu.CompilerParams(vmem_limit_bytes=vmem_bytes),
        cost_estimate=pl.CostEstimate(
            flops=0, bytes_accessed=4 * math.prod(shape), transcendentals=0
        ),
        name="cut",
    )(inner)


def pack_kernel(owned, part, row, target_ref, count_ref, inner_ref, out_ref, tile_ref, sems):
    rows = (out_ref.shape[0] - spare) // (inner_ref.shape[2] // lanes)
    start = pl.multiple_of(target_ref[0] * owned + row, spare)
    copies = [
        pltpu.make_async_copy(
            inner_ref.at[part, pl.ds(start, rows), pl.ds(j * lanes, lanes)],
            out_ref.at[pl.ds(j * rows, rows), :],
            sems.at[j],
        )
        for j in range(inner_ref.shape[2] // lanes)
    ]
    for copy in copies:
        copy.start()
    count = count_ref[0]
    high = (count >> 8).astype(jnp.float32)
    low = (count & 255).astype(jnp.float32)
    row = lax.broadcasted_iota(jnp.int32, tile_ref.shape, 0)
    tile_ref[...] = jnp.where(row == 0, high, low).astype(jnp.bfloat16)
    copies.append(
        pltpu.make_async_copy(
            tile_ref,
            out_ref.at[pl.ds(out_ref.shape[0] - spare, spare), :],
            sems.at[len(copies)],
        )
    )
    copies[-1].start()
    for copy in copies:
        copy.wait()


def pack(chunk, target, counts, inner, owned):
    part, row, rows = chunk.lo, chunk.row, chunk.rows
    blocks = inner.shape[2] // lanes
    scalar = pl.BlockSpec(memory_space=pltpu.SMEM)
    anywhere = pl.BlockSpec(memory_space=pl.ANY)
    return pl.pallas_call(
        functools.partial(pack_kernel, owned, part, row),
        in_specs=[scalar, scalar, anywhere],
        out_specs=anywhere,
        out_shape=jax.ShapeDtypeStruct((blocks * rows + spare, lanes), jnp.bfloat16),
        scratch_shapes=[
            pltpu.VMEM((spare, lanes), jnp.bfloat16),
            pltpu.SemaphoreType.DMA((blocks + 1,)),
        ],
        compiler_params=pltpu.CompilerParams(vmem_limit_bytes=vmem_bytes),
        cost_estimate=pl.CostEstimate(
            flops=0, bytes_accessed=4 * blocks * rows * lanes, transcendentals=0
        ),
        name="pack",
    )(target, counts, inner)


def share_kernel(mine_ref, *refs):
    tiles, shares_ref = refs[:-1], refs[-1]
    values = [mine_ref[0].astype(jnp.float32)]
    for ref in tiles:
        tile = ref[...].astype(jnp.float32)
        values.append(tile[0, 0] * 256.0 + tile[1, 0])
    total = values[0]
    for value in values[1:]:
        total = total + value
    for g, value in enumerate(values):
        shares_ref[g] = value / total


def share(counts, arrived):
    scalar = pl.BlockSpec(memory_space=pltpu.SMEM)
    last = arrived[0].shape[0] // spare - 1
    tile = pl.BlockSpec((spare, lanes), lambda i: (last, 0))
    return pl.pallas_call(
        share_kernel,
        grid=(1,),
        in_specs=[scalar] + [tile] * len(arrived),
        out_specs=scalar,
        out_shape=jax.ShapeDtypeStruct((1 + len(arrived),), jnp.float32),
        name="share",
    )(counts, *arrived)


def update_kernel(groups, me_ref, shares_ref, anchor_ref, inner_ref, *refs):
    arrived, momentum_ref = refs[: groups - 1], refs[groups - 1]
    new_ref, weights_ref, moments_ref = refs[-3:]
    base = anchor_ref[...].astype(jnp.float32)
    pseudo = shares_ref[0] * (base - inner_ref[...].astype(jnp.float32))
    for g, block_ref in enumerate(arrived, 1):
        block = block_ref[...].astype(jnp.float32).reshape(base.shape)
        pseudo = pseudo + shares_ref[g] * (base - block)
    moment = momentum_rate * momentum_ref[...] + pseudo
    new = (base - outer_rate * (pseudo + momentum_rate * moment)).astype(jnp.bfloat16)
    moments_ref[...] = moment
    weights_ref[...] = new
    new_ref[...] = new


def update(groups, chunk, me, shares, anchor, inner, arrived, momentum, held):
    _, owned, width = momentum.shape
    lo, row, rows = chunk.lo, chunk.row, chunk.rows
    if arrived[0].ndim == 2:
        grid = (1, width // lanes)
        block = (1, rows, lanes)
        ahead, mine = row // rows, owned // rows
        came = pl.BlockSpec((rows, lanes), lambda p, j, me_ref: (j, 0))
        packed = pl.BlockSpec(block, lambda p, j, me_ref: (0, 0, j))
        spread = pl.BlockSpec(block, lambda p, j, me_ref: (lo, me_ref[0] * mine + ahead, j))
        kept = pl.BlockSpec(block, lambda p, j, me_ref: (lo, ahead, j))
    else:
        tall = math.gcd(row, rows, owned, 128)
        grid = (chunk.parts, rows // tall)
        block = (1, tall, width)
        ahead, mine = row // tall, owned // tall
        came = pl.BlockSpec(block, lambda p, r, me_ref: (p, r, 0))
        packed = came
        spread = pl.BlockSpec(
            block, lambda p, r, me_ref: (lo + p, me_ref[0] * mine + ahead + r, 0)
        )
        kept = pl.BlockSpec(block, lambda p, r, me_ref: (lo + p, ahead + r, 0))
    scalar = pl.BlockSpec(memory_space=pltpu.SMEM)
    aliases = {groups + 4: 1, groups + 5: 2} if held else {}
    size = chunk.parts * rows * width
    return pl.pallas_call(
        functools.partial(update_kernel, groups),
        grid_spec=pltpu.PrefetchScalarGridSpec(
            num_scalar_prefetch=1,
            grid=grid,
            in_specs=[scalar, spread, spread]
            + [came] * (groups - 1)
            + [kept]
            + [pl.BlockSpec(memory_space=pl.ANY)] * len(held),
            out_specs=[packed, spread, kept],
        ),
        out_shape=[
            jax.ShapeDtypeStruct((chunk.parts, rows, width), jnp.bfloat16),
            jax.ShapeDtypeStruct(anchor.shape, jnp.bfloat16),
            jax.ShapeDtypeStruct(momentum.shape, jnp.float32),
        ],
        input_output_aliases=aliases,
        compiler_params=pltpu.CompilerParams(vmem_limit_bytes=vmem_bytes),
        cost_estimate=pl.CostEstimate(
            flops=12 * size, bytes_accessed=(14 + 2 * groups) * size, transcendentals=0
        ),
        name="update",
    )(me, shares, anchor, inner, *arrived, momentum, *held)


def place_kernel(groups, owned, chunk, shift, block_ref, _, weights_ref, sem):
    source = lax.rem(lax.axis_index("replica") + groups - shift, groups)
    start = pl.multiple_of(source * owned + chunk.row, spare)
    copy = pltpu.make_async_copy(
        block_ref, weights_ref.at[pl.ds(chunk.lo, chunk.parts), pl.ds(start, chunk.rows), :], sem
    )
    copy.start()
    copy.wait()


def place(groups, owned, chunk, shift, block, weights):
    anywhere = pl.BlockSpec(memory_space=pl.ANY)
    return pl.pallas_call(
        functools.partial(place_kernel, groups, owned, chunk, shift),
        in_specs=[anywhere, anywhere],
        out_specs=anywhere,
        out_shape=jax.ShapeDtypeStruct(weights.shape, weights.dtype),
        scratch_shapes=[pltpu.SemaphoreType.DMA],
        input_output_aliases={1: 0},
        compiler_params=pltpu.CompilerParams(vmem_limit_bytes=vmem_bytes),
        cost_estimate=pl.CostEstimate(flops=0, bytes_accessed=4 * block.size, transcendentals=0),
        name="place",
    )(block, weights)


def solution(mesh):
    groups = mesh.shape["replica"]

    def shifted(value, shift):
        pairs = [(i, (i + shift) % groups) for i in range(groups)]
        return lax.ppermute(value, "replica", pairs)

    def on_device(counts, inner, anchor, momentum):
        shape = anchor.shape
        owned, width = momentum.shape[-2:]
        parts = shape[0] * shape[1]
        inner = inner.reshape(parts, *shape[-2:])
        anchor = anchor.reshape(parts, *shape[-2:])
        momentum = momentum.reshape(parts, owned, width)
        me = lax.axis_index("replica")
        half = owned // 2
        chunks = [Chunk(0, 1, 0, half), Chunk(0, 1, half, half)]
        chunks += [Chunk(p, 1, 0, owned) for p in range(1, parts)]
        shifts = range(1, groups)

        def rows_for(array, chunk, target):
            sizes = (chunk.parts, chunk.rows, width)
            return lax.dynamic_slice(array, (chunk.lo, target * owned + chunk.row, 0), sizes)

        targets = [(me + s) % groups for s in shifts]
        first = [cut(groups, owned, chunks[0], s, inner) for s in shifts]
        first, rest, later_counts = lax.optimization_barrier((first, inner, counts))
        second = [
            pack(chunks[1], t.reshape(1).astype(jnp.int32), later_counts, rest, owned)
            for t in targets
        ]
        sent = [first, second] + [[rows_for(rest, c, t) for t in targets] for c in chunks[2:]]
        arrived = [[shifted(v, s) for v, s in zip(values, shifts)] for values in sent]
        shares = share(later_counts, arrived[1])

        where = me.reshape(1).astype(jnp.int32)
        held = []
        travelled = []
        for chunk, blocks in zip(chunks, arrived):
            new, *held = update(
                groups, chunk, where, shares, anchor, inner, blocks, momentum, held
            )
            travelled.append([shifted(new, s) for s in shifts])
        weights, moments = held
        for chunk, blocks in zip(chunks, travelled):
            for s, block in zip(shifts, blocks):
                weights = place(groups, owned, chunk, s, block, weights)
        return weights.reshape(shape), moments.reshape(*shape[:2], owned, width)

    placed = (
        P("replica"),
        P("replica", None, None, "fsdp", None),
        P(None, None, "fsdp", None),
        P(None, None, ("fsdp", "replica"), None),
    )
    return jax.shard_map(
        on_device,
        mesh=mesh,
        in_specs=placed,
        out_specs=(P(None, None, "fsdp", None), P(None, None, ("fsdp", "replica"), None)),
        check_vma=False,
    )
```
